32 devices in a mesh: dp: 4 (over x, core), row: 4 (over z), col: 2 (over y).
Axes of the slice: x: 2, y: 2, z: 4, core: 2. Of those that a mesh axis runs over, the one named last changes fastest.
Arguments:
- activations: float32 [4096, 2048], P(('dp', 'row'), 'col'), may hold values from -12 to 12
- ln_gain: float32 [2048], P('col'), may hold values from 0.1 to 1.9
- ln_bias: float32 [2048], P('col'), may hold values from -3 to 3
- w_query: bfloat16 [2048, 2048], P('col', 'row'), may hold values from -0.125 to 0.125
- w_key: bfloat16 [2048, 2048], P('col', 'row'), may hold values from -0.125 to 0.125
- w_value: bfloat16 [2048, 2048], P('col', 'row'), may hold values from -0.125 to 0.125
- b_query: float32 [2048], P(('row', 'col')), may hold values from -3 to 3
- b_key: float32 [2048], P(('row', 'col')), may hold values from -3 to 3
- b_value: float32 [2048], P(('row', 'col')), may hold values from -3 to 3
- w_out: bfloat16 [2048, 2048], P('row', 'col'), may hold values from -0.375 to 0.375
- w_up: bfloat16 [2048, 8192], P('col', 'row'), may hold values from -1 to 1
- b_up: float32 [8192], P(('row', 'col')), may hold values from -3 to 3
- w_down: bfloat16 [8192, 2048], P('row', 'col'), may hold values from -0.0625 to 0.0625
- out_bias: float32 [2048], P('col'), may hold values from -3 to 3
- grad_out: bfloat16 [4096, 2048], P('dp', 'col'), may hold values from -6 to 6
Outputs:
- block_out: float32 [4096, 2048], P(('dp', 'row'), 'col')
- grad_activations: float32 [4096, 2048], P(('dp', 'row'), 'col')
- grad_ln_gain: float32 [2048], P('col')
- grad_ln_bias: float32 [2048], P('col')
- grad_w_query: float32 [2048, 2048], P('col', 'row')
- grad_w_key: float32 [2048, 2048], P('col', 'row')
- grad_w_value: float32 [2048, 2048], P('col', 'row')
- grad_b_query: float32 [2048], P(('row', 'col'))
- grad_b_key: float32 [2048], P(('row', 'col'))
- grad_b_value: float32 [2048], P(('row', 'col'))
- grad_w_out: float32 [2048, 2048], P('row', 'col')
- grad_w_up: float32 [2048, 8192], P('col', 'row')
- grad_b_up: float32 [8192], P(('row', 'col'))
- grad_w_down: float32 [8192, 2048], P('row', 'col')
- grad_out_bias: float32 [2048], P('col')
The draws below stay inside these ranges and needn't reach their ends.
All inputs are finite; a program needn't handle non-finite values.
Results may differ from the reference program's by a relative error of at most 0.0093.
The reference program's roundings to bfloat16 on the way count: a program that leaves them out, or rounds other values in their place, can miss the bound.
Values may be sent and summed in bfloat16 or wider, within the bound.
No kernel may reach another device: no remote copies, remote signals or barrier semaphores. Data moves between devices by JAX's collectives and lax.ppermute only.
A program may use at most 192 MiB of HBM per device.

```python
import jax
import jax.numpy as jnp
from jax import lax

D = 2048
HEADS = 32
HEAD_DIM = 64
ROT = 32
FF = 8192
LEN = 1024
TOKENS = 4096


def draw_activations(key, part):
    key = jax.random.fold_in(key, 11)
    position = jnp.arange(D).astype(jnp.float32) / (D - 1)
    column_scale = 0.6 * jnp.exp(jnp.log(3.0) * position)
    noise = jnp.clip(jax.random.normal(key, (TOKENS, D), jnp.float32), -6.0, 6.0)
    return noise * column_scale[None, :]


def draw_w_up(key, part):
    key = jax.random.fold_in(key, 13)
    noise = jax.random.normal(key, (D, FF), jnp.float32)
    return (jnp.clip(noise, -6.0, 6.0) * D ** (-0.5)).astype(jnp.bfloat16)


def shard_levels(rng, extent, cuts, least, top_value):
    def one(dim, blocks):
        steps = jax.random.uniform(jax.random.fold_in(jax.random.fold_in(rng, 6), dim), (blocks,), jnp.float32, least / len(cuts), top_value / len(cuts))
        return jnp.repeat(jnp.exp(steps), extent[dim] // blocks).reshape((-1,) + (1,) * (len(extent) - dim - 1))

    gain = one(*cuts[0])
    for cut in cuts[1:]:
        gain = gain * one(*cut)
    return gain


def centred(own_key, extent, width, bound, shards=(), kind=jnp.bfloat16):
    drawn = width * jax.random.normal(own_key, extent, jnp.float32)
    if shards:
        drawn = drawn * shard_levels(own_key, extent, shards, -0.22, 0.18)
    return jnp.clip(drawn, -bound, bound).astype(kind)


def setup_inputs(seed: int = 0) -> dict:
    streams_of = jax.random.split(jax.random.key(seed), 16)
    return {
        "activations": draw_activations(jax.random.fold_in(streams_of[15], 71), 0),
        "ln_gain": jnp.clip(1.0 + 0.18 * jax.random.normal(streams_of[1], (D,), jnp.float32), 0.1, 1.9),
        "ln_bias": centred(streams_of[2], (D,), 0.3, 3.0, ((0, 2),), jnp.float32),
        "w_query": centred(streams_of[3], (D, D), D ** -0.5, 0.125, ((0, 2), (1, 4))),
        "w_key": centred(streams_of[4], (D, D), D ** -0.5, 0.125, ((0, 2), (1, 4))),
        "w_value": centred(streams_of[5], (D, D), D ** -0.5, 0.125, ((0, 2), (1, 4))),
        "b_query": centred(streams_of[6], (D,), 0.5, 3.0, ((0, 8),), jnp.float32),
        "b_key": centred(streams_of[7], (D,), 0.5, 3.0, ((0, 8),), jnp.float32),
        "b_value": centred(streams_of[8], (D,), 0.5, 3.0, ((0, 8),), jnp.float32),
        "w_out": centred(streams_of[9], (D, D), (D // 8) ** -0.5, 0.375, ((0, 4), (1, 2))),
        "w_up": draw_w_up(jax.random.fold_in(streams_of[15], 71), 0),
        "b_up": centred(streams_of[11], (FF,), 0.5, 3.0, ((0, 8),), jnp.float32),
        "w_down": centred(streams_of[12], (FF, D), FF ** -0.5, 0.0625, ((0, 4), (1, 2))),
        "out_bias": centred(streams_of[13], (D,), 0.5, 3.0, ((0, 2),), jnp.float32),
        "grad_out": centred(streams_of[14], (TOKENS, D), 1.0, 6.0, ((0, 4), (1, 2))),
    }


@jax.custom_vjp
def low(v):
    return lax.optimization_barrier(v.astype(jnp.bfloat16)).astype(jnp.float32)

@jax.custom_vjp
def low_back(v):
    return v

def low_keep(v):
    return (low(v), None)

def low_pass(kept, grad):
    return (grad,)

def back_keep(v):
    return (v, None)

def back_low(kept, grad):
    return (low(grad),)
low.defvjp(low_keep, low_pass)
low_back.defvjp(back_keep, back_low)
highest = lax.Precision.HIGHEST

def matmul(left_side, right_side):
    return jnp.dot(left_side, right_side, precision=highest)

def rotary_tables(positions):
    exponents = jnp.arange(0, ROT, 2).astype(jnp.float32) / ROT
    frequency = 10000.0 ** (-exponents)
    angles = positions.astype(jnp.float32)[:, None] * frequency[None, :]
    return (jnp.cos(angles), jnp.sin(angles))

def rotate(head_values, cosine, sine_table):
    half_width = ROT // 2
    leading = head_values[..., :half_width]
    trailing = head_values[..., half_width:ROT]
    cos_wide = cosine[:, None, :]
    sin_wide = sine_table[:, None, :]
    return jnp.concatenate([leading * cos_wide - trailing * sin_wide, trailing * cos_wide + leading * sin_wide, head_values[..., ROT:]], axis=-1)

def attend(triple):
    query_heads, key_heads, value_heads = triple
    scores = jnp.einsum('qhd,khd->hqk', query_heads, key_heads, precision=highest) * HEAD_DIM ** (-0.5)
    causal = jnp.arange(LEN)[:, None] >= jnp.arange(LEN)[None, :]
    scores = low_back(jnp.where(causal[None], scores, -1e+30))
    weights = low(jax.nn.softmax(scores, axis=-1))
    return jnp.einsum('hqk,khd->qhd', weights, value_heads, precision=highest)

def forward(activations, ln_gain, ln_bias, w_query, w_key, w_value, b_query, b_key, b_value, w_out, w_up, b_up, w_down, out_bias):
    tokens = activations.shape[0]
    average = lax.optimization_barrier(jnp.mean(activations, axis=-1, keepdims=True))
    variance = lax.optimization_barrier(jnp.mean(activations * activations, axis=-1, keepdims=True)) - average * average
    centered = (activations - average) * lax.rsqrt(variance + 1e-05)
    normed = low(centered * ln_gain + ln_bias)
    cosine, sine_table = rotary_tables(jnp.arange(tokens) % LEN)

    def split_heads(flat_values):
        return flat_values.reshape(tokens, HEADS, HEAD_DIM)
    query_heads = low(rotate(split_heads(low_back(matmul(normed, w_query) + b_query)), cosine, sine_table))
    key_heads = low(rotate(split_heads(low_back(matmul(normed, w_key) + b_key)), cosine, sine_table))
    value_heads = split_heads(low(low_back(matmul(normed, w_value) + b_value)))
    sequences = tokens // LEN

    def by_sequence(heads_array):
        return heads_array.reshape(sequences, LEN, HEADS, HEAD_DIM)
    attended = lax.map(jax.checkpoint(attend), (by_sequence(query_heads), by_sequence(key_heads), by_sequence(value_heads)))
    attended = low(low_back(attended.reshape(tokens, HEADS * HEAD_DIM)))
    hidden = low(jax.nn.gelu(low_back(matmul(normed, w_up) + b_up), approximate=True))
    return activations + matmul(attended, w_out) + matmul(hidden, w_down) + out_bias

def reference(activations, ln_gain, ln_bias, w_query, w_key, w_value, b_query, b_key, b_value, w_out, w_up, b_up, w_down, out_bias, grad_out):
    primals = tuple((argument.astype(jnp.float32) for argument in (activations, ln_gain, ln_bias, w_query, w_key, w_value, b_query, b_key, b_value, w_out, w_up, b_up, w_down, out_bias)))
    output, pullback = jax.vjp(forward, *primals)
    gradients = pullback(grad_out.astype(jnp.float32))
    return (output, gradients[0], gradients[1], gradients[2], gradients[3], gradients[4], gradients[5], gradients[6], gradients[7], gradients[8], gradients[9], gradients[10], gradients[11], gradients[12], gradients[13])
```

```python
import jax
import jax.numpy as jnp
from jax import lax
from jax.experimental import pallas as pl
from jax.experimental.pallas import tpu as pltpu
from jax.sharding import PartitionSpec as P

HEAD_DIM = 64
ROT = 32
LEN = 1024
BF16 = jnp.bfloat16
F32 = jnp.float32
TILE = 256
PAIR = 2 * HEAD_DIM


def rotary_rows(tokens):
    exponents = jnp.arange(0, ROT, 2).astype(F32) / ROT
    frequency = 10000.0 ** (-exponents)
    angles = (jnp.arange(tokens) % LEN).astype(F32)[:, None] * frequency[None, :]
    cosine, sine = jnp.cos(angles), jnp.sin(angles)
    half = ROT // 2
    none = jnp.zeros((tokens, half), F32)
    rest = jnp.zeros((tokens, HEAD_DIM - ROT), F32)
    own = jnp.concatenate([cosine, cosine, rest + 1.0] * 2, axis=1)
    ahead = jnp.concatenate([-sine, none, rest] * 2, axis=1)
    behind = jnp.concatenate([none, sine, rest] * 2, axis=1)
    return own, ahead, behind


def attention_kernel(
    pre_ref, bias_ref, go_ref, own_ref, ahead_ref, behind_ref,
    out_ref, grad_ref, sum_ref,
    q_ref, k_ref, v_ref, d_ref, dq_ref, dk_ref, dv_ref,
):
    half = ROT // 2
    rows = pre_ref.shape[0]
    own, ahead, behind = own_ref[...], ahead_ref[...], behind_ref[...]

    def turn(x):
        return x * own + pltpu.roll(x, PAIR - half, 1) * ahead + pltpu.roll(x, half, 1) * behind

    def turn_back(x):
        return x * own - pltpu.roll(x, PAIR - half, 1) * ahead - pltpu.roll(x, half, 1) * behind

    biased = [pre_ref[:, i * PAIR : (i + 1) * PAIR] + bias_ref[0, :, i * PAIR : (i + 1) * PAIR] for i in range(3)]
    query = turn(biased[0]).astype(BF16) * HEAD_DIM ** (-0.5)
    key = turn(biased[1]).astype(BF16)
    value = biased[2].astype(BF16)
    grad_out = go_ref[...]
    lane = lax.broadcasted_iota(jnp.int32, (rows, PAIR), 1)
    for head in range(2):
        mine = (lane >= head * HEAD_DIM) & (lane < (head + 1) * HEAD_DIM)
        for ref, array in ((q_ref, query), (k_ref, key), (v_ref, value), (d_ref, grad_out)):
            ref[head] = jnp.where(mine, array, jnp.zeros_like(array))
    nt = (((1,), (1,)), ((), ()))
    nn = (((1,), (0,)), ((), ()))
    tn = (((0,), (0,)), ((), ()))

    def dot(a, b, dims):
        return lax.dot_general(a, b, dims, preferred_element_type=F32)

    tiles = rows // TILE
    for i in reversed(range(tiles)):
        at = pl.ds(i * TILE, TILE)
        span = (i + 1) * TILE
        attended = None
        grad_query = None
        for head in range(2):
            q, d = q_ref[head, at], d_ref[head, at]
            k, v = k_ref[head, :span], v_ref[head, :span]
            scores = dot(q, k, nt)
            row = lax.broadcasted_iota(jnp.int32, (TILE, span), 0) + i * TILE
            col = lax.broadcasted_iota(jnp.int32, (TILE, span), 1)
            scores = jnp.where(row >= col, scores, -1e30)
            e = jnp.exp(scores - jnp.max(scores, axis=1, keepdims=True))
            p = e * (1.0 / jnp.sum(e, axis=1, keepdims=True))
            w = p.astype(BF16)
            gw = dot(d, v, nt)
            gs = (p * (gw - jnp.sum(p * gw, axis=1, keepdims=True))).astype(BF16)
            o = dot(w, v, nn)
            gq = dot(gs, k, nn)
            attended = o if attended is None else attended + o
            grad_query = gq if grad_query is None else grad_query + gq
            gv = dot(w, d, tn)
            gk = dot(gs, q, tn)
            if i == tiles - 1 and head == 0:
                dv_ref[...] = gv
                dk_ref[...] = gk
            else:
                dv_ref[:span] += gv
                dk_ref[:span] += gk
        out_ref[at] = attended.astype(BF16)
        dq_ref[at] = grad_query
    gq = turn_back(dq_ref[...] * HEAD_DIM ** (-0.5)).astype(BF16)
    gk = turn_back(dk_ref[...]).astype(BF16)
    gv = dv_ref[...].astype(BF16)
    for i, g in enumerate((gq, gk, gv)):
        grad_ref[:, i * PAIR : (i + 1) * PAIR] = g
        sum_ref[0, :, i * PAIR : (i + 1) * PAIR] = jnp.sum(g.astype(F32), axis=0, keepdims=True)


def attention(pre, bias, grad_out):
    rows, heads = pre.shape[0], grad_out.shape[1] // HEAD_DIM
    pairs = heads // 2
    wide = 3 * PAIR
    tables = rotary_rows(rows)
    whole = pl.BlockSpec((rows, PAIR), lambda j: (0, 0))
    out, grads, sums = pl.pallas_call(
        attention_kernel,
        grid=(pairs,),
        in_specs=[
            pl.BlockSpec((rows, wide), lambda j: (0, j)),
            pl.BlockSpec((1, 1, wide), lambda j: (j, 0, 0)),
            pl.BlockSpec((rows, PAIR), lambda j: (0, j)),
            whole, whole, whole,
        ],
        out_specs=[
            pl.BlockSpec((rows, PAIR), lambda j: (0, j)),
            pl.BlockSpec((rows, wide), lambda j: (0, j)),
            pl.BlockSpec((1, 1, wide), lambda j: (j, 0, 0)),
        ],
        out_shape=[
            jax.ShapeDtypeStruct((rows, pairs * PAIR), BF16),
            jax.ShapeDtypeStruct((rows, pairs * wide), BF16),
            jax.ShapeDtypeStruct((pairs, 1, wide), F32),
        ],
        scratch_shapes=[pltpu.VMEM((2, rows, PAIR), BF16)] * 4 + [pltpu.VMEM((rows, PAIR), F32)] * 3,
        compiler_params=pltpu.CompilerParams(
            dimension_semantics=("arbitrary",), vmem_limit_bytes=48 * 2**20
        ),
        cost_estimate=pl.CostEstimate(
            flops=12 * rows * rows * HEAD_DIM * heads,
            bytes_accessed=rows * pairs * wide * 8,
            transcendentals=rows * rows * heads // 2,
        ),
        name="attention",
    )(pre, bias.reshape(pairs, 1, wide), grad_out, *tables)
    return out, grads, sums.reshape(pairs * wide)


def swap(array, axis, bit=0):
    size = lax.axis_size(axis)
    return lax.ppermute(array, axis, [(i, i ^ (1 << bit)) for i in range(size)])


def step_up(array):
    size = lax.axis_size("row")
    return lax.ppermute(array, "row", [(i, (i + 1) % size) for i in range(size)])


def part(array, index, parts, dim=0):
    size = array.shape[dim] // parts
    return lax.dynamic_slice_in_dim(array, index * size, size, dim)


def ordered(bit, mine, other, dim):
    return jnp.where(
        bit == 0, jnp.concatenate([mine, other], dim), jnp.concatenate([other, mine], dim)
    )


def dot(a, b, left, right):
    return lax.dot_general(a, b, (((left,), (right,)), ((), ())), preferred_element_type=F32)


def gather_rows(own):
    size = lax.axis_size("row")
    rows = own.shape[0]
    here = lax.axis_index("row")
    whole = jnp.zeros((size * rows,) + own.shape[1:], own.dtype)
    whole = lax.dynamic_update_slice_in_dim(whole, own, here * rows, 0)
    block = own
    for step in range(1, size):
        block = step_up(block)
        whole = lax.dynamic_update_slice_in_dim(whole, block, (here - step) % size * rows, 0)
    return whole


def scatter_rows(whole):
    size = lax.axis_size("row")
    here = lax.axis_index("row")
    total = None
    for step in range(1, size + 1):
        block = part(whole, (here - step) % size, size).astype(F32)
        if total is not None:
            block = block + total.astype(F32)
        if step < size:
            total = step_up(block.astype(BF16))
    return block


def partner_block(send, places):
    bits = min(2, lax.axis_size("dp").bit_length() - 1)
    index = 0
    for bit in range(bits):
        index = index * 2 + places[bit]
    block = swap(part(send, index, 1 << bits), "col")
    for bit in reversed(range(bits)):
        block = ordered(places[bit], block, swap(block, "dp", bit), 0)
    return block


def total_grads(own, other, places):
    both = jnp.stack([own, other])
    bits = len(places)
    for bit in range(bits):
        keep = part(both, places[bit], 2, 1)
        send = part(both, 1 - places[bit], 2, 1)
        both = (keep.astype(F32) + swap(send, "dp", bit).astype(F32)).astype(BF16)
    both = jnp.stack([both[0], swap(both[1], "col")])
    for bit in reversed(range(bits)):
        both = ordered(places[bit], both, swap(both, "dp", bit), 1)
    return both[0].astype(F32), both[1].astype(F32)


def gelu_tanh(pre_values):
    return jax.nn.gelu(pre_values, approximate=True)


def body(
    activations,
    ln_gain,
    ln_bias,
    w_query,
    w_key,
    w_value,
    b_query,
    b_key,
    b_value,
    w_out,
    w_up,
    b_up,
    w_down,
    out_bias,
    grad_out,
):
    dp, row, col = (lax.axis_index(axis) for axis in ("dp", "row", "col"))
    places = [(dp >> bit) & 1 for bit in range(lax.axis_size("dp").bit_length() - 1)]
    own_rows = activations.shape[0]
    feature_count = activations.shape[1] * lax.axis_size("col")

    local = jnp.stack(
        [jnp.sum(activations, axis=1), jnp.sum(activations * activations, axis=1)]
    )
    moments = local + swap(local, "col")
    average = moments[0] / feature_count
    variance = moments[1] / feature_count - average * average
    inverse = lax.rsqrt(variance + 1e-05)[:, None]
    centered = (activations - average[:, None]) * inverse
    normed = (centered * ln_gain + ln_bias).astype(BF16)

    def columns(which):
        halves = []
        for w in (w_query, w_key, w_value):
            mine = part(w, which, 2, 1)
            halves.append(mine.reshape(mine.shape[0], -1, PAIR))
        return jnp.stack(halves, axis=2).reshape(w_query.shape[0], -1)

    up_own = part(w_up, col, 2, 1)
    up_other = partner_block(part(w_up, 1 - col, 2, 1), places)
    normed_own = gather_rows(normed)
    normed_other = gather_rows(swap(normed, "col"))
    qkv_own = columns(col)
    qkv_other = partner_block(columns(1 - col), places)
    grad_other = swap(grad_out, "col")
    down_own = part(w_down, col, 2, 0)
    down_other = partner_block(part(w_down, 1 - col, 2, 0), places)
    out_own = part(w_out, col, 2, 0)
    out_other = partner_block(part(w_out, 1 - col, 2, 0), places)

    hidden_pre = dot(normed_own, up_own, 1, 0) + dot(normed_other, up_other, 1, 0)
    hidden_full, gelu_back = jax.vjp(gelu_tanh, hidden_pre + b_up)
    hidden = hidden_full.astype(BF16)
    grad_hidden = dot(grad_out, down_own, 1, 1) + dot(grad_other, down_other, 1, 1)
    grad_pre = gelu_back(grad_hidden)[0].astype(BF16)
    grad_down = total_grads(
        dot(hidden, grad_out, 0, 0).astype(BF16), dot(hidden, grad_other, 0, 0).astype(BF16), places
    )
    grad_up = total_grads(
        dot(normed_own, grad_pre, 0, 0).astype(BF16),
        dot(normed_other, grad_pre, 0, 0).astype(BF16),
        places,
    )

    qkv_pre = dot(normed_own, qkv_own, 1, 0) + dot(normed_other, qkv_other, 1, 0)
    bias = jnp.stack([b.reshape(-1, PAIR) for b in (b_query, b_key, b_value)], axis=1).reshape(-1)
    grad_attended = (dot(grad_out, out_own, 1, 1) + dot(grad_other, out_other, 1, 1)).astype(BF16)
    attended, grad_qkv, grad_bias = attention(qkv_pre, bias, grad_attended)

    grad_attn = total_grads(
        jnp.concatenate(
            [dot(normed_own, grad_qkv, 0, 0), dot(grad_out, attended, 0, 0)], axis=1
        ).astype(BF16),
        jnp.concatenate(
            [dot(normed_other, grad_qkv, 0, 0), dot(grad_other, attended, 0, 0)], axis=1
        ).astype(BF16),
        places,
    )

    mixed_own = dot(hidden, down_own, 1, 0) + dot(attended, out_own, 1, 0)
    mixed_other = dot(hidden, down_other, 1, 0) + dot(attended, out_other, 1, 0)
    mixed_own = scatter_rows(mixed_own)
    mixed_other = scatter_rows(mixed_other)
    block_out = (
        activations + (mixed_own + swap(mixed_other.astype(BF16), "col").astype(F32)) + out_bias
    )

    normed_grad_own = dot(grad_pre, up_own, 1, 1) + dot(grad_qkv, qkv_own, 1, 1)
    normed_grad_other = dot(grad_pre, up_other, 1, 1) + dot(grad_qkv, qkv_other, 1, 1)
    normed_grad_own = scatter_rows(normed_grad_own)
    normed_grad_other = scatter_rows(normed_grad_other)
    grad_normed = normed_grad_own + swap(normed_grad_other.astype(BF16), "col").astype(F32)

    scaled = grad_normed * ln_gain
    local = jnp.stack([jnp.sum(scaled, axis=1), jnp.sum(scaled * centered, axis=1)])
    back_moments = (local + swap(local, "col")) / feature_count
    own_grad = part(grad_out, row, lax.axis_size("row")).astype(F32)
    grad_activations = own_grad + inverse * (
        scaled - back_moments[0][:, None] - centered * back_moments[1][:, None]
    )
    grad_ln = lax.psum(
        jnp.stack([jnp.sum(grad_normed * centered, axis=0), jnp.sum(grad_normed, axis=0)]),
        ("dp", "row"),
    )
    widths = [grad_bias.shape[0], b_up.shape[0]]
    sums = lax.psum(
        jnp.concatenate(
            [
                grad_bias,
                jnp.sum(grad_pre, axis=0, dtype=F32),
                jnp.sum(grad_out, axis=0, dtype=F32),
            ]
        ),
        "dp",
    )
    grad_bias, grad_b_up, grad_out_bias = jnp.split(sums, [widths[0], sum(widths)])
    grad_bias = grad_bias.reshape(-1, 3, PAIR)


    wide = grad_qkv.shape[1]
    qkv_pieces = [piece[:, :wide].reshape(piece.shape[0], -1, 3, PAIR) for piece in grad_attn]
    grad_w_qkv = [
        ordered(col, *(piece[:, :, i].reshape(piece.shape[0], -1) for piece in qkv_pieces), 1)
        for i in range(3)
    ]
    grad_w_out = ordered(col, *(piece[:, wide:].T for piece in grad_attn), 0)
    return (
        block_out,
        grad_activations,
        grad_ln[0],
        grad_ln[1],
        grad_w_qkv[0],
        grad_w_qkv[1],
        grad_w_qkv[2],
        grad_bias[:, 0].reshape(-1),
        grad_bias[:, 1].reshape(-1),
        grad_bias[:, 2].reshape(-1),
        grad_w_out,
        ordered(col, *grad_up, 1),
        grad_b_up,
        ordered(col, *grad_down, 0),
        grad_out_bias,
    )


def solution(mesh):
    placed = (
        P(("dp", "row"), "col"),
        P("col"),
        P("col"),
        P("col", "row"),
        P("col", "row"),
        P("col", "row"),
        P(("row", "col")),
        P(("row", "col")),
        P(("row", "col")),
        P("row", "col"),
        P("col", "row"),
        P(("row", "col")),
        P("row", "col"),
        P("col"),
        P("dp", "col"),
    )
    return jax.shard_map(
        body,
        mesh=mesh,
        in_specs=placed,
        out_specs=(
            P(("dp", "row"), "col"),
            P(("dp", "row"), "col"),
            P("col"),
            P("col"),
            P("col", "row"),
            P("col", "row"),
            P("col", "row"),
            P(("row", "col")),
            P(("row", "col")),
            P(("row", "col")),
            P("row", "col"),
            P("col", "row"),
            P(("row", "col")),
            P("row", "col"),
            P("col"),
        ),
        check_vma=False,
    )
```

```python
import jax
import jax.numpy as jnp
import numpy as np
from jax import lax
from jax.experimental import pallas as pl
from jax.experimental.pallas import tpu as pltpu
from jax.sharding import PartitionSpec as P

HEAD_DIM = 64
ROT = 32
LEN = 1024
BF16 = jnp.bfloat16
F32 = jnp.float32
TILE = 256
PAIR = 2 * HEAD_DIM
NN = (((1,), (0,)), ((), ()))
NT = (((1,), (1,)), ((), ()))
TN = (((0,), (0,)), ((), ()))
WORK = dict.fromkeys(("join_up", "join_heads", "hidden_units", "outer", "take_half", "carry"), 0)


def mul(a, b, dims):
    return lax.dot_general(a, b, dims, preferred_element_type=F32)


def whole(shape):
    return pl.BlockSpec(shape, lambda *_: (0,) * len(shape))


def call(kernel, name, grid, in_specs, out_specs, out_shape, scratch=(), prefetch=0, vmem=60, after=(), aliases={}):
    given = prefetch + len(in_specs)

    def without(*refs):
        kernel(*refs[:given], *refs[given + len(after) :])

    function = pl.pallas_call(
        without,
        grid_spec=pltpu.PrefetchScalarGridSpec(
            num_scalar_prefetch=prefetch,
            grid=grid,
            in_specs=in_specs + [pl.BlockSpec(memory_space=pl.ANY)] * len(after),
            out_specs=out_specs,
            scratch_shapes=scratch,
        ),
        out_shape=[jax.ShapeDtypeStruct(*pair) for pair in out_shape],
        input_output_aliases=aliases,
        compiler_params=pltpu.CompilerParams(
            dimension_semantics=("arbitrary",) * len(grid), vmem_limit_bytes=vmem * 2**20
        ),
        cost_estimate=pl.CostEstimate(
            flops=WORK.get(name, 100_000_000_000), bytes_accessed=200_000_000, transcendentals=0
        ),
        name=name,
    )
    return lambda *arguments: function(*arguments, *after)


def cut_pieces(places, w_up, w_down, w_query, w_key, w_value, w_out):
    features = w_up.shape[0]
    rows = features // 2
    units = w_up.shape[1] // 4
    wide = 3 * PAIR
    height = PAIR // 2

    def kernel(p_ref, up_ref, down_ref, q_ref, k_ref, v_ref, out_ref, early_ref, third_ref):
        early_ref[:rows] = up_ref[...]
        third_ref[...] = down_ref[...]
        for i, ref in enumerate((q_ref, k_ref, v_ref)):
            early_ref[rows:, i * PAIR : (i + 1) * PAIR] = ref[...]
        for i in range(rows // height):
            at = rows + i * height
            early_ref[at : at + height, wide:] = out_ref[:, i * PAIR : (i + 1) * PAIR]

    def across(width):
        return pl.BlockSpec((rows, width), lambda i, p: (p[1], 2 * (1 - p[2]) + p[0]))

    def down(size):
        return pl.BlockSpec((size, features), lambda i, p: (4 * (1 - p[2]) + 2 * p[0] + p[1], 0))

    shapes = [(2 * rows, units), (units // 2, features)]
    return call(
        kernel,
        "cut_pieces",
        (1,),
        [across(units), down(units // 2), across(PAIR), across(PAIR), across(PAIR), down(height)],
        [whole(shape) for shape in shapes],
        [(shape, BF16) for shape in shapes],
        prefetch=1,
    )(places, w_up, w_down, w_query, w_key, w_value, w_out)


def at_half(places_ref, j, size):
    return pl.ds(pl.multiple_of((places_ref[1] ^ j) * size, size), size)


def join_up(places, w_up, pieces, after=()):
    features = w_up.shape[0]
    rows, units = pieces[0].shape[0] // 2, pieces[0].shape[1]

    def kernel(places_ref, near_ref, *refs):
        up_ref = refs[2]
        up_ref[:features] = near_ref[...]
        for j in range(2):
            up_ref[pl.ds(pl.multiple_of(features + (places_ref[1] ^ j) * rows, rows), rows), :] = refs[j][...]

    return call(
        kernel,
        "join_up",
        (1,),
        [pl.BlockSpec((features, units), lambda i, p: (0, 2 * p[2] + p[0]))]
        + [pl.BlockSpec((rows, units), lambda i, p: (0, 0))] * 2,
        [whole((2 * features, units))],
        [((2 * features, units), BF16)],
        prefetch=1,
        after=after,
    )(places, w_up, *pieces)[0]


def join_down(places, w_down, pieces, after=()):
    rows, features = pieces[0].shape

    def kernel(places_ref, *refs):
        for j in range(2):
            refs[2][at_half(places_ref, j, rows), :] = refs[j][...]

    return call(
        kernel,
        "join_down",
        (1,),
        [whole(a.shape) for a in pieces],
        [whole((2 * rows, features))],
        [((2 * rows, features), BF16)],
        prefetch=1,
        after=after,
    )(places, *pieces)[0]


def join_heads(places, w_query, w_key, w_value, pieces, after=()):
    features = w_query.shape[0]
    rows, width = pieces[0].shape[0] // 2, pieces[0].shape[1]
    wide = 3 * PAIR
    height = PAIR // 2

    def kernel(places_ref, q_ref, k_ref, v_ref, mine_ref, over_ref, qkv_ref, far_ref):
        for i, ref in enumerate((q_ref, k_ref, v_ref)):
            qkv_ref[:features, i * PAIR : (i + 1) * PAIR] = ref[...]

        def write(x):
            for j, ref in enumerate((mine_ref, over_ref)):
                at = x ^ j
                qkv_ref[features + at * rows : features + (at + 1) * rows, :] = ref[:, :wide]
                for i in range(rows // height):
                    far_ref[at * height : (at + 1) * height, i * PAIR : (i + 1) * PAIR] = ref[
                        i * height : (i + 1) * height, wide:
                    ]

        for x in range(2):
            pl.when(places_ref[1] == x)(lambda x=x: write(x))

    column = pl.BlockSpec((features, PAIR), lambda i, p: (0, 2 * p[2] + p[0]))
    shapes = [(2 * features, wide), (PAIR, features)]
    return call(
        kernel,
        "join_heads",
        (1,),
        [column, column, column] + [pl.BlockSpec((rows, width), lambda i, p: (1, 0))] * 2,
        [whole(shape) for shape in shapes],
        [(shape, BF16) for shape in shapes],
        prefetch=1,
        after=after,
    )(places, w_query, w_key, w_value, *pieces)


def token_block(row_ref, count, step):
    return lax.rem(row_ref[0] + 2 * count - step, count)


def hidden_units(row, count, size, steps, blocks, w, b, earlier, after=()):
    features = blocks[0][0].shape[1]
    depth, width = w.shape
    number = 2 * len(steps)

    def kernel(row_ref, *refs):
        x_refs, refs = refs[: 2 * number], refs[2 * number :]
        w_ref, b_ref, (x_ref, hidden_ref, slope_ref) = refs[0], refs[1], refs[-3:]
        for i in range(number):

            @pl.when(pl.program_id(0) == i)
            def _(i=i):
                x_ref[:, :features] = x_refs[2 * i][...]
                x_ref[:, features:] = x_refs[2 * i + 1][...]

        u = mul(x_ref[...], w_ref[...], NN) + b_ref[...]
        scale = (2.0 / np.pi) ** 0.5
        square = u * u
        t = jnp.tanh(scale * u * (1.0 + 0.044715 * square))
        half = 0.5 * (1.0 + t)
        hidden_ref[...] = (u * half).astype(BF16)
        slope_ref[...] = half + 0.5 * u * (1.0 - t * t) * scale * (1.0 + 3 * 0.044715 * square)

    def at(i, row_ref):
        return (i % 2 * count + token_block(row_ref, count, steps[0] + i // 2), 0)

    rows = 2 * count * size
    shapes = [((rows, depth), BF16), ((rows, width), BF16), ((rows, width), F32)]
    return call(
        kernel,
        "hidden_units",
        (number,),
        [pl.BlockSpec((size, features), lambda i, r, n=n: (n, 0)) for _, n in blocks]
        + [whole((depth, width)), whole((1, width))]
        + [pl.BlockSpec(memory_space=pl.ANY)] * len(earlier),
        [pl.BlockSpec((size, shape[1]), at) for shape, _ in shapes],
        shapes,
        prefetch=1,
        after=after,
        aliases={3 + len(blocks) + i: i for i in range(len(earlier))},
    )(row, *(array for array, _ in blocks), w, b.reshape(1, -1), *earlier)


def take_half(both, after=()):
    size, width = both.shape[0] // 2, both.shape[1]

    def kernel(in_ref, out_ref):
        out_ref[...] = in_ref[...]

    return call(
        kernel,
        "take_half",
        (1,),
        [pl.BlockSpec((size, width), lambda i: (1, 0))],
        [whole((size, width))],
        [((size, width), BF16)],
        after=after,
    )(both)[0]


def outer(places, a, grads, after=()):
    rows, width = grads[0].shape
    units = a.shape[1]
    half = units // 2

    def kernel(places_ref, a0_ref, a1_ref, b0_ref, b1_ref, kept_ref, sent_ref):
        total = (mul(a0_ref[...], b0_ref[...], TN) + mul(a1_ref[...], b1_ref[...], TN)).astype(BF16)
        for x in range(2):

            @pl.when(places_ref[1] == x)
            def _(x=x):
                kept_ref[...] = total[x * half : (x + 1) * half]
                sent_ref[...] = total[(1 - x) * half : (2 - x) * half]

    return call(
        kernel,
        "outer",
        (1,),
        [pl.BlockSpec((rows, units), lambda i, p, s=s: (s, 0)) for s in range(2)]
        + [whole((rows, width))] * 2,
        [whole((half, width))] * 2,
        [((half, width), BF16)] * 2,
        prefetch=1,
        after=after,
    )(places, a, a, *grads)


def keep_tile(places_ref, i, total, near_ref, far_ref, sent_ref):
    total = total.astype(BF16)

    @pl.when(places_ref[1] == i % 2)
    def _():
        (near_ref, far_ref)[i // 2][...] = total

    @pl.when(places_ref[1] != i % 2)
    def _():
        sent_ref[i // 2] = total


def hidden_back(places, near, far, w_down, w_far, slope, x, after=()):
    rows, features = near[0].shape
    units = w_far.shape[0]
    size = rows // 2
    steps = 2 * rows // size
    tile = x.shape[1] // 4

    def kernel(places_ref, n0, n1, f0, f1, wn_ref, wf_ref, slope_ref, x_hbm, pre_ref, sum_ref, *refs):
        outs, (x_ref, sem) = refs[:-2], refs[-2:]
        i = pl.program_id(0)
        fetch = pltpu.make_async_copy(x_hbm, x_ref, sem)

        @pl.when(i == 0)
        def _():
            fetch.start()
            sum_ref[...] = jnp.zeros_like(sum_ref)

        def write(near_ref, far_ref):
            g = mul(near_ref[...], wn_ref[...], NT) + mul(far_ref[...], wf_ref[...], NT)
            g = (g * slope_ref[...]).astype(BF16)
            pre_ref[pl.ds(pl.multiple_of(i * size, size), size), :] = g
            sum_ref[...] += jnp.sum(g.astype(F32), axis=0, keepdims=True)

        pl.when(i < steps // 2)(lambda: write(n0, f0))
        pl.when(i >= steps // 2)(lambda: write(n1, f1))

        @pl.when(i == steps - 1)
        def _():
            fetch.wait()
            for j in range(4):
                keep_tile(places_ref, j, mul(x_ref[:, j * tile : (j + 1) * tile], pre_ref[...], TN), *outs)

    first = pl.BlockSpec((size, features), lambda i, p: (jnp.minimum(i, steps // 2 - 1), 0))
    second = pl.BlockSpec((size, features), lambda i, p: (jnp.maximum(i - steps // 2, 0), 0))
    shapes = [(tile, units), (tile, units), (2, tile, units)]
    return call(
        kernel,
        "hidden_back",
        (steps,),
        [first, second, first, second]
        + [pl.BlockSpec((units, features), lambda i, p: (2 * p[2] + p[0], 0)), whole(w_far.shape)]
        + [pl.BlockSpec((size, units), lambda i, p: (i, 0)), pl.BlockSpec(memory_space=pl.ANY)],
        [whole((2 * rows, units)), whole((1, units))] + [whole(shape) for shape in shapes],
        [((2 * rows, units), BF16), ((1, units), F32)] + [(shape, BF16) for shape in shapes],
        scratch=[pltpu.VMEM(x.shape, BF16), pltpu.SemaphoreType.DMA],
        prefetch=1,
        after=after,
    )(places, *near, *far, w_down, w_far, slope, x)


def write_blocks(row_ref, count, block, scratch_ref, out_ref):
    size = out_ref.shape[0] // count
    scratch_ref[...] = block.astype(BF16)
    for i in range(count):
        at = token_block(row_ref, count, 1 + i) * size
        out_ref[i * size : (i + 1) * size] = scratch_ref[pl.ds(pl.multiple_of(at, size), size), :]


def back_to_tokens(row, count, side, pre, grads, up, qkv, after=()):
    rows = grads[0].shape[0]
    features = up.shape[0] // 2
    units, wide = pre.shape[1], grads[0].shape[1]
    depth = units + wide
    tile = 2 * TILE
    tiles = features // tile

    def kernel(row_ref, p0, p1, g0, g1, up_ref, qkv_ref, theirs_ref, own_ref, x_ref, w_ref, scratch_ref):
        w_ref[:, :units] = up_ref[...]
        w_ref[:, units:] = qkv_ref[...]
        for s, (p, g, out_ref) in enumerate(((p1, g1, theirs_ref), (p0, g0, own_ref))):

            @pl.when(pl.program_id(0) == 0)
            def _(s=s, p=p, g=g):
                x_ref[s, :, :units] = p[...]
                x_ref[s, :, units:] = g[...]

            write_blocks(row_ref, count, mul(x_ref[s], w_ref[...], NT), scratch_ref, out_ref)

    return call(
        kernel,
        "back_to_tokens",
        (tiles,),
        [pl.BlockSpec((rows, units), lambda i, r, s=s: (s, 0)) for s in range(2)]
        + [whole(g.shape) for g in grads]
        + [pl.BlockSpec((tile, w.shape[1]), lambda i, r: (side * tiles + i, 0)) for w in (up, qkv)],
        [pl.BlockSpec((rows, tile), lambda i, r: (0, i))] * 2,
        [((rows, features), BF16)] * 2,
        scratch=[
            pltpu.VMEM((2, rows, depth), BF16),
            pltpu.VMEM((tile, depth), BF16),
            pltpu.VMEM((rows, tile), BF16),
        ],
        prefetch=1,
        after=after,
    )(row, pre, pre, *grads, up, qkv)


def mix(row, places, count, sequence, hidden, attended, w_down, down_far, w_out, out_far, after=()):
    units, features = down_far.shape
    rows = hidden.shape[0] // 2
    heads = out_far.shape[0]
    tile = 2 * TILE
    tiles = features // tile
    depth = units + heads

    def kernel(row_ref, p_ref, h_ref, a_ref, dn_ref, df_ref, on_ref, of_ref, out_ref, x_ref, w_ref, scratch_ref):
        i = pl.program_id(0)

        @pl.when(i == 0)
        def _():
            x_ref[:, :units] = h_ref[...]
            x_ref[:, units:] = a_ref[...]

        @pl.when(i < tiles)
        def _():
            w_ref[:units] = dn_ref[...]
            w_ref[units:] = on_ref[...]

        @pl.when(i >= tiles)
        def _():
            w_ref[:units] = df_ref[...]
            w_ref[units:] = of_ref[...]

        write_blocks(row_ref, count, mul(x_ref[...], w_ref[...], NN), scratch_ref, out_ref)

    def near(height):
        return pl.BlockSpec((height, tile), lambda i, r, p: (2 * p[2] + p[0], jnp.minimum(i, tiles - 1)))

    def far(height):
        return pl.BlockSpec((height, tile), lambda i, r, p: (0, jnp.maximum(i - tiles, 0)))

    return call(
        kernel,
        "mix",
        (2 * tiles,),
        [pl.BlockSpec((rows, units), lambda i, r, p: (sequence, 0)), whole(attended.shape)]
        + [near(units), far(units), near(heads), far(heads)],
        [pl.BlockSpec((rows, tile), lambda i, r, p: (0, i))],
        [((rows, 2 * features), BF16)],
        scratch=[
            pltpu.VMEM((rows, depth), BF16),
            pltpu.VMEM((depth, tile), BF16),
            pltpu.VMEM((rows, tile), BF16),
        ],
        prefetch=2,
        after=after,
    )(row, places, hidden, attended, w_down, down_far, w_out, out_far)[0]


def add_blocks(kind, size, width, *terms, after=()):
    terms = [(*term, 0)[:3] for term in terms]

    def kernel(*refs):
        total = refs[0][...].astype(F32)
        for ref in refs[1:-1]:
            total = total + ref[...].astype(F32)
        refs[-1][...] = total.astype(kind)

    return call(
        kernel,
        "add_blocks",
        (1,),
        [pl.BlockSpec((size, width), lambda i, n=n, m=m: (n, m)) for _, n, m in terms],
        [whole((size, width))],
        [((size, width), kind)],
        after=after,
    )(*(array for array, _, _ in terms))[0]


def add_half(width, column, half, a, b, after=()):
    size = a.shape[0] // 4

    def kernel(a_ref, b_ref, out_ref):
        out_ref[...] = (a_ref[...].astype(F32) + b_ref[...].astype(F32)).astype(BF16)

    block = pl.BlockSpec((size, width), lambda i: (2 * half + i, column))
    return call(
        kernel,
        "add_half",
        (2,),
        [block, block],
        [pl.BlockSpec((size, width), lambda i: (i, 0))],
        [((2 * size, width), BF16)],
        after=after,
    )(a, b)[0]


def add_up(kind, *terms, after=()):
    def kernel(*refs):
        total = refs[0][...].astype(F32)
        for ref in refs[1:-1]:
            total = total + ref[...].astype(F32)
        refs[-1][...] = total.astype(kind)

    shape = terms[0].shape
    return call(
        kernel, "add_up", (1,), [whole(shape)] * len(terms), [whole(shape)], [(shape, kind)], after=after
    )(*terms)[0]


def add_pairs(kept, got, after=()):
    def kernel(near_ref, far_ref, got_ref, near_out, far_out):
        for i, (ref, out) in enumerate(((near_ref, near_out), (far_ref, far_out))):
            out[...] = (ref[...].astype(F32) + got_ref[i].astype(F32)).astype(BF16)

    shape = kept[0].shape
    return call(
        kernel,
        "add_pairs",
        (1,),
        [whole(shape), whole(shape), whole(got.shape)],
        [whole(shape)] * 2,
        [(shape, BF16)] * 2,
        after=after,
    )(*kept, got)


def rotary_rows(tokens):
    exponents = np.arange(0, ROT, 2).astype(np.float32) / np.float32(ROT)
    frequency = np.float32(10000.0) ** (-exponents)
    angles = (np.arange(tokens) % LEN).astype(np.float32)[:, None] * frequency[None, :]
    cosine, sine = np.cos(angles), np.sin(angles)
    none = np.zeros((tokens, ROT // 2), np.float32)
    rest = np.zeros((tokens, HEAD_DIM - ROT), np.float32)
    own = np.concatenate([cosine, cosine, rest + 1.0] * 2, axis=1)
    ahead = np.concatenate([-sine, none, rest] * 2, axis=1)
    behind = np.concatenate([none, sine, rest] * 2, axis=1)
    return tuple(table.astype(np.float32) for table in (own, ahead, behind))


def attention_kernel(
    sequence, places_ref, x_hbm, w_ref, bias_ref, near_ref, far_ref, on_ref, of_ref, own_ref, ahead_ref, behind_ref,
    *refs,
):
    *refs, x_ref, x_sem, q_ref, k_ref, v_ref, d_ref, dq_ref, dk_ref, dv_ref = refs
    got_ref = refs[0] if len(refs) == 7 else None
    out_ref, grad_ref, sum_ref, *weight_refs = refs if got_ref is None else refs[1:]
    half = ROT // 2
    rows, features = near_ref.shape
    own, ahead, behind = own_ref[...], ahead_ref[...], behind_ref[...]
    fetch = pltpu.make_async_copy(x_hbm.at[pl.ds(sequence * rows, rows)], x_ref, x_sem)
    fetch.start()

    def turn(x):
        return x * own + pltpu.roll(x, PAIR - half, 1) * ahead + pltpu.roll(x, half, 1) * behind

    def turn_back(x):
        return x * own - pltpu.roll(x, PAIR - half, 1) * ahead - pltpu.roll(x, half, 1) * behind

    grad_out = mul(near_ref[...], on_ref[...], NT) + mul(far_ref[...], of_ref[...], NT)
    grad_out = grad_out.astype(BF16)
    fetch.wait()
    pre = mul(x_ref[...], w_ref[...], NN) + bias_ref[...]
    biased = [pre[:, i * PAIR : (i + 1) * PAIR] for i in range(3)]
    query = turn(biased[0]).astype(BF16) * HEAD_DIM ** (-0.5)
    key = turn(biased[1]).astype(BF16)
    value = biased[2].astype(BF16)
    lane = lax.broadcasted_iota(jnp.int32, (rows, PAIR), 1)
    for head in range(2):
        mine = (lane >= head * HEAD_DIM) & (lane < (head + 1) * HEAD_DIM)
        for ref, array in ((q_ref, query), (k_ref, key), (v_ref, value), (d_ref, grad_out)):
            ref[head] = jnp.where(mine, array, jnp.zeros_like(array))

    tiles = rows // TILE
    for i in reversed(range(tiles)):
        at = pl.ds(i * TILE, TILE)
        span = (i + 1) * TILE
        attended = None
        grad_query = None
        for head in range(2):
            q, d = q_ref[head, at], d_ref[head, at]
            k, v = k_ref[head, :span], v_ref[head, :span]
            scores = mul(q, k, NT)
            row = lax.broadcasted_iota(jnp.int32, (TILE, span), 0) + i * TILE
            col = lax.broadcasted_iota(jnp.int32, (TILE, span), 1)
            scores = jnp.where(row >= col, scores, -1e30)
            e = jnp.exp(scores - jnp.max(scores, axis=1, keepdims=True))
            p = e * (1.0 / jnp.sum(e, axis=1, keepdims=True))
            w = p.astype(BF16)
            gw = mul(d, v, NT)
            gs = (p * (gw - jnp.sum(p * gw, axis=1, keepdims=True))).astype(BF16)
            o = mul(w, v, NN)
            gq = mul(gs, k, NN)
            attended = o if attended is None else attended + o
            grad_query = gq if grad_query is None else grad_query + gq
            gv = mul(w, d, TN)
            gk = mul(gs, q, TN)
            if i == tiles - 1 and head == 0:
                dv_ref[...] = gv
                dk_ref[...] = gk
            else:
                dv_ref[:span] += gv
                dk_ref[:span] += gk
        out_ref[at] = attended.astype(BF16)
        dq_ref[at] = grad_query
    gq = turn_back(dq_ref[...] * HEAD_DIM ** (-0.5)).astype(BF16)
    gk = turn_back(dk_ref[...]).astype(BF16)
    gv = dv_ref[...].astype(BF16)
    for i, g in enumerate((gq, gk, gv)):
        grad_ref[:, i * PAIR : (i + 1) * PAIR] = g
        sum_ref[:, i * PAIR : (i + 1) * PAIR] = jnp.sum(g.astype(F32), axis=0, keepdims=True)
    tile = 2 * features // 4
    for i in range(4):
        at = i * tile
        source = near_ref if at < features else far_ref
        block = jnp.concatenate(
            [
                mul(x_ref[:, at : at + tile], grad_ref[...], TN),
                mul(source[:, at % features : at % features + tile], out_ref[...], TN),
            ],
            axis=1,
        )
        if got_ref is None:
            weight_refs[0][at : at + tile] = block
        else:
            keep_tile(places_ref, i, block + got_ref[at : at + tile], *weight_refs)


def attention(places, sequence, x, qkv, bias, near, far, w_out, out_far, earlier=None, after=()):
    rows, features = near.shape
    wide = 3 * PAIR
    tables = [jnp.asarray(table) for table in rotary_rows(rows)]
    tile = 2 * features // 4
    earlier = [] if earlier is None else [earlier]
    if earlier:
        shapes = [((tile, 4 * PAIR), BF16)] * 2 + [((2, tile, 4 * PAIR), BF16)]
    else:
        shapes = [((4 * tile, 4 * PAIR), F32)]

    def kernel(*refs):
        attention_kernel(sequence, *refs)

    return call(
        kernel,
        "attention",
        (1,),
        [
            pl.BlockSpec(memory_space=pl.ANY),
            whole(qkv.shape),
            whole((1, wide)),
            whole(near.shape),
            whole(far.shape),
            pl.BlockSpec((PAIR, features), lambda i, p: (2 * p[2] + p[0], 0)),
            whole(out_far.shape),
        ]
        + [whole((rows, PAIR))] * 3
        + [whole(a.shape) for a in earlier],
        [whole((rows, PAIR)), whole((rows, wide)), whole((1, wide))] + [whole(shape) for shape, _ in shapes],
        [((rows, PAIR), BF16), ((rows, wide), BF16), ((1, wide), F32)] + shapes,
        scratch=[pltpu.VMEM((rows, 2 * features), BF16), pltpu.SemaphoreType.DMA]
        + [pltpu.VMEM((2, rows, PAIR), BF16)] * 4
        + [pltpu.VMEM((rows, PAIR), F32)] * 3,
        prefetch=1,
        after=after,
    )(places, x, qkv, bias.reshape(1, -1), near, far, w_out, out_far, *tables, *earlier)


def carry(array, after=()):
    def kernel(in_ref, out_ref):
        out_ref[...] = in_ref[...]

    half = pl.BlockSpec((array.shape[0] // 2, array.shape[1]), lambda i: (i, 0))
    return call(kernel, "carry", (2,), [half], [half], [(array.shape, array.dtype)], after=after)(array)[0]


def pair_up(first, second, after=()):
    shape = (2, *first.shape)

    def kernel(first_ref, second_ref, out_ref):
        for i, ref in enumerate((first_ref, second_ref)):

            @pl.when(pl.program_id(0) == i)
            def _(ref=ref):
                out_ref[0] = ref[...]

    return call(
        kernel,
        "pair_up",
        (2,),
        [whole(first.shape), whole(second.shape)],
        [pl.BlockSpec((1, *first.shape), lambda i: (i, 0, 0))],
        [(shape, first.dtype)],
        after=after,
    )(first, second)[0]


def place_kernel(places_ref, *refs):
    sources, targets = refs[:4], refs[4:]
    sibling, across, side = (pl.program_id(i) for i in range(3))
    for i in range(4):

        @pl.when((sibling == i // 2) & (across == i % 2))
        def _(source=sources[i]):
            block = source[side].astype(F32)
            if len(targets) == 1:
                targets[0][...] = block
            else:
                for t in range(3):
                    targets[t][...] = block[:, t * PAIR : (t + 1) * PAIR]
                targets[3][...] = block[:, 3 * PAIR :].T


def place(places, sources, blocks, shapes, maps, after=()):
    def spec(block, index):
        return pl.BlockSpec(block, lambda i, j, s, p: index(p[0] ^ i, p[1] ^ j, p[2] ^ s))

    return call(
        place_kernel,
        "place",
        (2, 2, 2),
        [whole(source.shape) for source in sources],
        [spec(*pair) for pair in zip(blocks, maps)],
        [(shape, F32) for shape in shapes],
        prefetch=1,
        after=after,
    )(places, *sources)


def swap(array, axis, bit=0, name="pieces"):
    size = lax.axis_size(axis)
    with jax.named_scope(name):
        return lax.ppermute(array, axis, [(i, i ^ (1 << bit)) for i in range(size)])


def step_up(array, name="row_ring"):
    size = lax.axis_size("row")
    with jax.named_scope(name):
        return lax.ppermute(array, "row", [(i, (i + 1) % size) for i in range(size)])


def part(array, index, parts, dim=0):
    size = array.shape[dim] // parts
    return lax.dynamic_slice_in_dim(array, index * size, size, dim)


def halves(array, dim):
    return jnp.split(array, 2, dim)


def pick(bit, first, second):
    return jnp.where(bit == 0, first, second)


def ordered(bit, mine, other, dim):
    return pick(bit, jnp.concatenate([mine, other], dim), jnp.concatenate([other, mine], dim))


def sync(*arrays):
    return lax.optimization_barrier(arrays)


def held(array, *others):
    return lax.optimization_barrier((array, *others))[0]


def add(a, b):
    return (a.astype(F32) + b.astype(F32)).astype(BF16)


def body(
    activations,
    ln_gain,
    ln_bias,
    w_query,
    w_key,
    w_value,
    b_query,
    b_key,
    b_value,
    w_out,
    w_up,
    b_up,
    w_down,
    out_bias,
    grad_out,
):
    dp, row, col = (lax.axis_index(axis) for axis in ("dp", "row", "col"))
    rows = lax.axis_size("row")
    bits = lax.axis_size("dp").bit_length() - 1
    places = [(dp >> bit) & 1 for bit in range(2)]
    where = jnp.stack([places[0], places[1], col]).astype(jnp.int32)
    here = row.reshape(1).astype(jnp.int32)
    own_rows, features = activations.shape
    feature_count = features * lax.axis_size("col")

    local = jnp.stack([jnp.sum(activations, axis=1), jnp.sum(activations * activations, axis=1)])
    early, third = cut_pieces(where, w_up, w_down, w_query, w_key, w_value, w_out)
    moments, early, third = sync(swap(local, "col"), early, third)
    moments = local + moments
    average = moments[0] / feature_count
    variance = moments[1] / feature_count - average * average
    inverse = lax.rsqrt(variance + 1e-05)[:, None]
    centered = (activations - average[:, None]) * inverse
    own = (centered * ln_gain + ln_bias).astype(BF16)

    def over_core(array, name="core"):
        return swap(array, "dp", 0, name)

    def over_x(array, name):
        return swap(array, "dp", 1, name)

    def over_col(array, name):
        return swap(array, "col", 0, name)

    near = [grad_out, over_core(grad_out, "grad_out")]
    own1 = step_up(own)
    other0 = over_col(own, "normed")
    early, other0 = sync(early, other0)
    early = over_col(early, "early")
    own2 = step_up(own1)
    front = jnp.concatenate([own, own1], 0)
    behind = jnp.concatenate([own2, other0], 0)
    ahead = step_up(behind)

    pieces = [early, over_x(early, "early")]
    up = join_up(where, w_up, pieces, after=near[1:])
    carried = carry(grad_out, after=[early])
    far = over_col(carried, "grad_out")
    other2 = step_up(take_half(ahead, after=[carried, up]))
    qkv, out_far = join_heads(where, w_query, w_key, w_value, pieces)
    third = over_col(third, "third")

    bias = [pick(places[0], *halves(b, 0)) for b in (b_query, b_key, b_value)]
    bias = jnp.concatenate(bias, 0)
    bias_up = pick(places[0], *halves(b_up, 0))

    front_sibling, behind_sibling, ahead_sibling = (
        over_core(a, "normed") for a in (front, behind, ahead)
    )
    blocks = [(front, 0), (behind, 1), (front_sibling, 0), (behind_sibling, 1)]
    blocks += [(front, 1), (ahead, 1), (front_sibling, 1), (ahead_sibling, 1)]
    normed, hidden, slope = hidden_units(
        here, rows, own_rows, range(2), blocks, up, bias_up, [], after=[qkv]
    )
    other2, hidden = sync(other2, hidden)
    other3 = step_up(other2)
    for step, mine, late in ((2, behind, other2), (3, ahead, other3)):
        sibling = behind_sibling if step == 2 else ahead_sibling
        blocks = [(mine, 0), (late, 0), (sibling, 0), (over_core(late, "normed"), 0)]
        normed, hidden, slope = hidden_units(
            here, rows, own_rows, range(step, step + 1), blocks, up, bias_up, [normed, hidden, slope]
        )

    def rest(total):
        for bit in range(2, bits):
            total = add(total, swap(total, "dp", bit))
        return total

    last = [hidden]

    def then(function, *arguments, pins=()):
        result = function(*arguments, after=[last[0], *pins])
        last[0] = jax.tree.leaves(result)[0]
        return result

    def plus(*terms, kind=BF16, pins=()):
        return then(lambda after: add_blocks(kind, own_rows, features, *terms, after=after), pins=pins)

    def plus_pairs(kept, got, pins=()):
        return [rest(total) for total in then(add_pairs, kept, got, pins=pins)]

    def attend(sequence, *arguments, pins=()):
        return then(
            lambda *a, after: attention(where, sequence, *a, after=after),
            normed, qkv, bias, near[sequence], far[sequence], w_out, out_far, *arguments, pins=pins,
        )

    def back(side, pins=()):
        return then(
            lambda *a, after: back_to_tokens(here, rows, side, *a, after=after),
            pre, qkv_grads, up, qkv, pins=pins,
        )

    def put(near, far, name, blocks, shapes, maps):
        pair = then(pair_up, near, far)
        across = over_x(pair, name)
        sources = [pair, across]

        def send():
            *sources[:], last[0] = sync(*sources, last[0])
            sources.extend(over_core(array, name) for array in sources[:])

        def write():
            return then(lambda *a, after: place(where, a, blocks, shapes, maps, after=after), *sources)

        return send, write, across

    near_keep, near_send = then(lambda *a, after: outer(where, *a, after=after), hidden, near)
    near_got = over_x(near_send, "down_near")

    far, last[0] = sync(far, last[0])
    far = [far, over_core(far, "grad_out")]
    attended0, grads0, sums0, weights = attend(0)
    third, last[0] = sync(third, last[0])
    third_across = over_x(third, "third")
    far_keep, far_send = then(lambda *a, after: outer(where, *a, after=after), hidden, far, pins=[near_got])
    far_got = over_x(far_send, "down_far")
    attended1, grads1, sums1, keep0, keep1, attn_send = attend(1, weights)
    attn_got = over_x(attn_send, "attn")
    qkv_grads = [grads0, grads1]

    near_total = rest(plus((near_keep, 0), (near_got, 0)))
    far_total = rest(plus((far_keep, 0), (far_got, 0)))
    far_mine = over_col(far_total, "down_far_col")
    down_far = then(lambda *a, after: join_down(where, *a, after=after), w_down, [third, third_across])

    def mixed_terms(sequence, attended, pins=()):
        return then(
            lambda *a, after: mix(here, where, rows, sequence, *a, after=after),
            hidden, attended, w_down, down_far, w_out, out_far, pins=pins,
        )

    theirs = over_core(mixed_terms(1, attended1), "block_out")
    mixed = mixed_terms(0, attended0, pins=[far_mine])
    send_down, put_down, down_across = put(
        near_total, far_mine,
        "down_back",
        [near_total.shape],
        [w_down.shape],
        [lambda k, x, c: (c * 4 + k * 2 + x, 0)],
    )
    attn_total = plus_pairs([keep0, keep1], attn_got)
    attn_mine = over_col(attn_total[1], "attn_far_col")

    def far_half(half, columns, own_terms, theirs, name):
        return over_col(
            then(lambda *a, after: add_half(features, columns, half, *a, after=after), own_terms, theirs), name
        )

    out_first = far_half(0, 1, mixed, theirs, "block_out_col")

    pre, sum_up, up0, up1, up_send = then(
        lambda *a, after: hidden_back(where, *a, after=after), near, far, w_down, down_far, slope, normed
    )
    up_got = over_x(up_send, "up")

    near_terms, near_own = back(0, pins=[down_across, attn_mine])
    near_terms = over_core(near_terms, "grad_normed")
    far_terms, far_own = back(1)
    far_terms = over_core(far_terms, "grad_normed")
    mixed_next = step_up(plus((mixed, 0), (theirs, 0), (out_first, 0)), "block_out_ring")
    far_first = far_half(0, 0, far_own, far_terms, "grad_normed_col")
    send_down()
    up_total = plus_pairs([up0, up1], up_got)
    far_second = far_half(1, 0, far_own, far_terms, "grad_normed_col")
    mixed_next = step_up(
        plus((mixed, 1), (theirs, 1), (out_first, 1), (mixed_next, 0)), "block_out_ring"
    )
    (grad_w_down,) = put_down()
    total = plus((near_own, 0), (near_terms, 0), (far_first, 0))
    total = step_up(total, "grad_normed_ring")
    up_mine = over_col(up_total[1], "up_far_col")
    send_attn, put_attn, attn_across = put(
        attn_total[0], attn_mine,
        "attn_back",
        [attn_mine.shape[:1] + (PAIR,)] * 3 + [(PAIR,) + attn_mine.shape[:1]],
        [w_query.shape, w_key.shape, w_value.shape, w_out.shape],
        [lambda k, x, c: (x, c * 2 + k)] * 3 + [lambda k, x, c: (c * 2 + k, x)],
    )
    total = plus((near_own, 1), (near_terms, 1), (far_first, 1), (total, 0))
    total = step_up(total, "grad_normed_ring")
    out_second = far_half(1, 1, mixed, theirs, "block_out_col")
    send_up, put_up, up_across = put(
        up_total[0], up_mine,
        "up_back",
        [up_mine.shape],
        [w_up.shape],
        [lambda k, x, c: (x, c * 2 + k)],
    )
    send_attn()
    total = plus((near_own, 2), (near_terms, 2), (far_second, 0), (total, 0))
    total = step_up(total, "grad_normed_ring")
    grad_w_query, grad_w_key, grad_w_value, grad_w_out = put_attn()
    grad_normed = plus((near_own, 3), (near_terms, 3), (far_second, 1), (total, 0), kind=F32)
    mixed_next = step_up(
        plus((mixed, 2), (theirs, 2), (out_second, 0), (mixed_next, 0)), "block_out_ring"
    )
    send_up()
    (grad_w_up,) = put_up()
    mixed_sum = plus((mixed, 3), (theirs, 3), (out_second, 1), (mixed_next, 0), kind=F32)

    def over_all(array, axis, name):
        bits = lax.axis_size(axis).bit_length() - 1
        size = lax.axis_size(axis)
        for bit in range(0, bits, 2):
            masks = [1 << bit, 2 << bit, 3 << bit] if bit + 1 < bits else [1 << bit]
            with jax.named_scope(name):
                got = [lax.ppermute(array, axis, [(i, i ^ mask) for i in range(size)]) for mask in masks]
            array = array + got[0]
            if len(got) == 3:
                array = array + (got[1] + got[2])
        return array

    scaled = grad_normed * ln_gain
    local = jnp.stack([jnp.sum(scaled, axis=1), jnp.sum(scaled * centered, axis=1)])
    back_moments = (local + swap(local, "col", 0, "moments")) / feature_count
    own_grad = part(grad_out, row, rows).astype(F32)
    grad_activations = own_grad + inverse * (
        scaled - back_moments[0][:, None] - centered * back_moments[1][:, None]
    )
    grad_ln = jnp.stack([jnp.sum(grad_normed * centered, axis=0), jnp.sum(grad_normed, axis=0)])
    grad_ln = over_all(grad_ln, "row", "ln_row")
    sums = jnp.concatenate([sums0 + sums1, sum_up], 1)
    grad_out_bias = jnp.sum(grad_out, axis=0, dtype=F32)
    sums, grad_out_bias, grad_ln = sync(sums, grad_out_bias, grad_ln)
    sums = ordered(places[0], sums, swap(sums, "dp", 0, "sums"), 0)
    grad_out_bias = grad_out_bias + swap(grad_out_bias, "dp", 0, "sums")
    sums = jnp.concatenate([sums.reshape(-1), grad_out_bias])
    for bit in range(1, bits):
        sums = sums + swap(sums, "dp", bit, "sums")
    grad_out_bias = sums[-features:]
    sums = sums[:-features].reshape(2, -1)
    grad_bias = [sums[:, i * PAIR : (i + 1) * PAIR].reshape(-1) for i in range(3)]
    grad_b_up = sums[:, 3 * PAIR :].reshape(-1)

    grad_ln = over_all(grad_ln, "dp", "ln_dp")
    block_out = activations + mixed_sum + out_bias

    return (
        block_out,
        grad_activations,
        grad_ln[0],
        grad_ln[1],
        grad_w_query,
        grad_w_key,
        grad_w_value,
        *grad_bias,
        grad_w_out,
        grad_w_up,
        grad_b_up,
        grad_w_down,
        grad_out_bias,
    )


def solution(mesh):
    placed = (
        P(("dp", "row"), "col"),
        P("col"),
        P("col"),
        P("col", "row"),
        P("col", "row"),
        P("col", "row"),
        P(("row", "col")),
        P(("row", "col")),
        P(("row", "col")),
        P("row", "col"),
        P("col", "row"),
        P(("row", "col")),
        P("row", "col"),
        P("col"),
        P("dp", "col"),
    )
    return jax.shard_map(
        body,
        mesh=mesh,
        in_specs=placed,
        out_specs=(
            P(("dp", "row"), "col"),
            P(("dp", "row"), "col"),
            P("col"),
            P("col"),
            P("col", "row"),
            P("col", "row"),
            P("col", "row"),
            P(("row", "col")),
            P(("row", "col")),
            P(("row", "col")),
            P("row", "col"),
            P("col", "row"),
            P(("row", "col")),
            P("row", "col"),
            P("col"),
        ),
        check_vma=False,
    )
```

```python
import jax
import jax.numpy as jnp
import numpy as np
from jax import lax
from jax.experimental import pallas as pl
from jax.experimental.pallas import tpu as pltpu
from jax.sharding import PartitionSpec as P

HEAD_DIM = 64
ROT = 32
LEN = 1024
BF16 = jnp.bfloat16
F32 = jnp.float32
TILE = 256
PAIR = 2 * HEAD_DIM
NN = (((1,), (0,)), ((), ()))
NT = (((1,), (1,)), ((), ()))
TN = (((0,), (0,)), ((), ()))
LARGE = 100_000_000_000
WORK = dict.fromkeys(("join_up", "join_heads", "hidden_units", "outer", "take_half", "carry"), 0)
SAID = [LARGE]


def mul(a, b, dims):
    return lax.dot_general(a, b, dims, preferred_element_type=F32)


def whole(shape):
    return pl.BlockSpec(shape, lambda *_: (0,) * len(shape))


def call(kernel, name, grid, in_specs, out_specs, out_shape, scratch=(), prefetch=0, vmem=60, after=(), aliases={}):
    given = prefetch + len(in_specs)

    def without(*refs):
        kernel(*refs[:given], *refs[given + len(after) :])

    function = pl.pallas_call(
        without,
        grid_spec=pltpu.PrefetchScalarGridSpec(
            num_scalar_prefetch=prefetch,
            grid=grid,
            in_specs=in_specs + [pl.BlockSpec(memory_space=pl.ANY)] * len(after),
            out_specs=out_specs,
            scratch_shapes=scratch,
        ),
        out_shape=[jax.ShapeDtypeStruct(*pair) for pair in out_shape],
        input_output_aliases=aliases,
        compiler_params=pltpu.CompilerParams(
            dimension_semantics=("arbitrary",) * len(grid), vmem_limit_bytes=vmem * 2**20
        ),
        cost_estimate=pl.CostEstimate(
            flops=WORK.get(name, SAID[0]), bytes_accessed=200_000_000, transcendentals=0
        ),
        name=name,
    )
    return lambda *arguments: function(*arguments, *after)


def cut_pieces(places, w_up, w_down, w_query, w_key, w_value, w_out):
    features = w_up.shape[0]
    rows = features // 2
    units = w_up.shape[1] // 4
    wide = 3 * PAIR
    height = PAIR // 2

    def kernel(p_ref, up_ref, down_ref, q_ref, k_ref, v_ref, out_ref, early_ref, third_ref):
        early_ref[:rows] = up_ref[...]
        third_ref[...] = down_ref[...]
        for i, ref in enumerate((q_ref, k_ref, v_ref)):
            early_ref[rows:, i * PAIR : (i + 1) * PAIR] = ref[...]
        for i in range(rows // height):
            at = rows + i * height
            early_ref[at : at + height, wide:] = out_ref[:, i * PAIR : (i + 1) * PAIR]

    def across(width):
        return pl.BlockSpec((rows, width), lambda i, p: (p[1], 2 * (1 - p[2]) + p[0]))

    def down(size):
        return pl.BlockSpec((size, features), lambda i, p: (4 * (1 - p[2]) + 2 * p[0] + p[1], 0))

    shapes = [(2 * rows, units), (units // 2, features)]
    return call(
        kernel,
        "cut_pieces",
        (1,),
        [across(units), down(units // 2), across(PAIR), across(PAIR), across(PAIR), down(height)],
        [whole(shape) for shape in shapes],
        [(shape, BF16) for shape in shapes],
        prefetch=1,
    )(places, w_up, w_down, w_query, w_key, w_value, w_out)


def at_half(places_ref, j, size):
    return pl.ds(pl.multiple_of((places_ref[1] ^ j) * size, size), size)


def join_up(places, w_up, pieces, after=()):
    features = w_up.shape[0]
    rows, units = pieces[0].shape[0] // 2, pieces[0].shape[1]

    def kernel(places_ref, near_ref, *refs):
        up_ref = refs[2]
        up_ref[:features] = near_ref[...]
        for j in range(2):
            up_ref[pl.ds(pl.multiple_of(features + (places_ref[1] ^ j) * rows, rows), rows), :] = refs[j][...]

    return call(
        kernel,
        "join_up",
        (1,),
        [pl.BlockSpec((features, units), lambda i, p: (0, 2 * p[2] + p[0]))]
        + [pl.BlockSpec((rows, units), lambda i, p: (0, 0))] * 2,
        [whole((2 * features, units))],
        [((2 * features, units), BF16)],
        prefetch=1,
        after=after,
    )(places, w_up, *pieces)[0]


def join_down(places, w_down, pieces, after=()):
    rows, features = pieces[0].shape

    def kernel(places_ref, *refs):
        for j in range(2):
            refs[2][at_half(places_ref, j, rows), :] = refs[j][...]

    return call(
        kernel,
        "join_down",
        (1,),
        [whole(a.shape) for a in pieces],
        [whole((2 * rows, features))],
        [((2 * rows, features), BF16)],
        prefetch=1,
        after=after,
    )(places, *pieces)[0]


def join_heads(places, w_query, w_key, w_value, pieces, after=()):
    features = w_query.shape[0]
    rows, width = pieces[0].shape[0] // 2, pieces[0].shape[1]
    wide = 3 * PAIR
    height = PAIR // 2

    def kernel(places_ref, q_ref, k_ref, v_ref, mine_ref, over_ref, qkv_ref, far_ref):
        for i, ref in enumerate((q_ref, k_ref, v_ref)):
            qkv_ref[:features, i * PAIR : (i + 1) * PAIR] = ref[...]

        def write(x):
            for j, ref in enumerate((mine_ref, over_ref)):
                at = x ^ j
                qkv_ref[features + at * rows : features + (at + 1) * rows, :] = ref[:, :wide]
                for i in range(rows // height):
                    far_ref[at * height : (at + 1) * height, i * PAIR : (i + 1) * PAIR] = ref[
                        i * height : (i + 1) * height, wide:
                    ]

        for x in range(2):
            pl.when(places_ref[1] == x)(lambda x=x: write(x))

    column = pl.BlockSpec((features, PAIR), lambda i, p: (0, 2 * p[2] + p[0]))
    shapes = [(2 * features, wide), (PAIR, features)]
    return call(
        kernel,
        "join_heads",
        (1,),
        [column, column, column] + [pl.BlockSpec((rows, width), lambda i, p: (1, 0))] * 2,
        [whole(shape) for shape in shapes],
        [(shape, BF16) for shape in shapes],
        prefetch=1,
        after=after,
    )(places, w_query, w_key, w_value, *pieces)


def token_block(row_ref, count, step):
    return lax.rem(row_ref[0] + 2 * count - step, count)


def hidden_units(row, count, size, steps, blocks, w, b, earlier, after=()):
    features = blocks[0][0].shape[1]
    depth, width = w.shape
    number = 2 * len(steps)

    def kernel(row_ref, *refs):
        x_refs, refs = refs[: 2 * number], refs[2 * number :]
        w_ref, b_ref, (x_ref, hidden_ref, slope_ref) = refs[0], refs[1], refs[-3:]
        for i in range(number):

            @pl.when(pl.program_id(0) == i)
            def _(i=i):
                x_ref[:, :features] = x_refs[2 * i][...]
                x_ref[:, features:] = x_refs[2 * i + 1][...]

        u = mul(x_ref[...], w_ref[...], NN) + b_ref[...]
        scale = (2.0 / np.pi) ** 0.5
        square = u * u
        t = jnp.tanh(scale * u * (1.0 + 0.044715 * square))
        half = 0.5 * (1.0 + t)
        hidden_ref[...] = (u * half).astype(BF16)
        slope_ref[...] = half + 0.5 * u * (1.0 - t * t) * scale * (1.0 + 3 * 0.044715 * square)

    def at(i, row_ref):
        return (i % 2 * count + token_block(row_ref, count, steps[0] + i // 2), 0)

    rows = 2 * count * size
    shapes = [((rows, depth), BF16), ((rows, width), BF16), ((rows, width), F32)]
    return call(
        kernel,
        "hidden_units",
        (number,),
        [pl.BlockSpec((size, features), lambda i, r, n=n: (n, 0)) for _, n in blocks]
        + [whole((depth, width)), whole((1, width))]
        + [pl.BlockSpec(memory_space=pl.ANY)] * len(earlier),
        [pl.BlockSpec((size, shape[1]), at) for shape, _ in shapes],
        shapes,
        prefetch=1,
        after=after,
        aliases={3 + len(blocks) + i: i for i in range(len(earlier))},
    )(row, *(array for array, _ in blocks), w, b.reshape(1, -1), *earlier)


def take_half(both, after=()):
    size, width = both.shape[0] // 2, both.shape[1]

    def kernel(in_ref, out_ref):
        out_ref[...] = in_ref[...]

    return call(
        kernel,
        "take_half",
        (1,),
        [pl.BlockSpec((size, width), lambda i: (1, 0))],
        [whole((size, width))],
        [((size, width), BF16)],
        after=after,
    )(both)[0]


def outer(places, a, grads, after=()):
    rows, width = grads[0].shape
    units = a.shape[1]
    half = units // 2

    def kernel(places_ref, a0_ref, a1_ref, b0_ref, b1_ref, kept_ref, sent_ref):
        total = (mul(a0_ref[...], b0_ref[...], TN) + mul(a1_ref[...], b1_ref[...], TN)).astype(BF16)
        for x in range(2):

            @pl.when(places_ref[1] == x)
            def _(x=x):
                kept_ref[...] = total[x * half : (x + 1) * half]
                sent_ref[...] = total[(1 - x) * half : (2 - x) * half]

    return call(
        kernel,
        "outer",
        (1,),
        [pl.BlockSpec((rows, units), lambda i, p, s=s: (s, 0)) for s in range(2)]
        + [whole((rows, width))] * 2,
        [whole((half, width))] * 2,
        [((half, width), BF16)] * 2,
        prefetch=1,
        after=after,
    )(places, a, a, *grads)


def keep_tile(places_ref, i, total, near_ref, far_ref, sent_ref):
    total = total.astype(BF16)

    @pl.when(places_ref[1] == i % 2)
    def _():
        (near_ref, far_ref)[i // 2][...] = total

    @pl.when(places_ref[1] != i % 2)
    def _():
        sent_ref[i // 2] = total


def hidden_back(places, near, far, w_down, w_far, slope, x, after=()):
    rows, features = near[0].shape
    units = w_far.shape[0]
    size = rows // 2
    steps = 2 * rows // size
    tile = x.shape[1] // 4

    def kernel(places_ref, n0, n1, f0, f1, wn_ref, wf_ref, slope_ref, x_hbm, pre_ref, sum_ref, *refs):
        outs, (x_ref, sem) = refs[:-2], refs[-2:]
        i = pl.program_id(0)
        fetch = pltpu.make_async_copy(x_hbm, x_ref, sem)

        @pl.when(i == 0)
        def _():
            fetch.start()
            sum_ref[...] = jnp.zeros_like(sum_ref)

        def write(near_ref, far_ref):
            g = mul(near_ref[...], wn_ref[...], NT) + mul(far_ref[...], wf_ref[...], NT)
            g = (g * slope_ref[...]).astype(BF16)
            pre_ref[pl.ds(pl.multiple_of(i * size, size), size), :] = g
            sum_ref[...] += jnp.sum(g.astype(F32), axis=0, keepdims=True)

        pl.when(i < steps // 2)(lambda: write(n0, f0))
        pl.when(i >= steps // 2)(lambda: write(n1, f1))

        @pl.when(i == steps - 1)
        def _():
            fetch.wait()
            for j in range(4):
                keep_tile(places_ref, j, mul(x_ref[:, j * tile : (j + 1) * tile], pre_ref[...], TN), *outs)

    first = pl.BlockSpec((size, features), lambda i, p: (jnp.minimum(i, steps // 2 - 1), 0))
    second = pl.BlockSpec((size, features), lambda i, p: (jnp.maximum(i - steps // 2, 0), 0))
    shapes = [(tile, units), (tile, units), (2, tile, units)]
    return call(
        kernel,
        "hidden_back",
        (steps,),
        [first, second, first, second]
        + [pl.BlockSpec((units, features), lambda i, p: (2 * p[2] + p[0], 0)), whole(w_far.shape)]
        + [pl.BlockSpec((size, units), lambda i, p: (i, 0)), pl.BlockSpec(memory_space=pl.ANY)],
        [whole((2 * rows, units)), whole((1, units))] + [whole(shape) for shape in shapes],
        [((2 * rows, units), BF16), ((1, units), F32)] + [(shape, BF16) for shape in shapes],
        scratch=[pltpu.VMEM(x.shape, BF16), pltpu.SemaphoreType.DMA],
        prefetch=1,
        after=after,
    )(places, *near, *far, w_down, w_far, slope, x)


def write_blocks(row_ref, count, block, scratch_ref, out_ref):
    size = out_ref.shape[0] // count
    scratch_ref[...] = block.astype(BF16)
    for i in range(count):
        at = token_block(row_ref, count, 1 + i) * size
        out_ref[i * size : (i + 1) * size] = scratch_ref[pl.ds(pl.multiple_of(at, size), size), :]


def back_to_tokens(row, count, side, pre, grads, up, qkv, after=()):
    rows = grads[0].shape[0]
    features = up.shape[0] // 2
    units, wide = pre.shape[1], grads[0].shape[1]
    depth = units + wide
    tile = 2 * TILE
    tiles = features // tile

    def kernel(row_ref, p0, p1, g0, g1, up_ref, qkv_ref, theirs_ref, own_ref, x_ref, w_ref, scratch_ref):
        w_ref[:, :units] = up_ref[...]
        w_ref[:, units:] = qkv_ref[...]
        for s, (p, g, out_ref) in enumerate(((p1, g1, theirs_ref), (p0, g0, own_ref))):

            @pl.when(pl.program_id(0) == 0)
            def _(s=s, p=p, g=g):
                x_ref[s, :, :units] = p[...]
                x_ref[s, :, units:] = g[...]

            write_blocks(row_ref, count, mul(x_ref[s], w_ref[...], NT), scratch_ref, out_ref)

    return call(
        kernel,
        "back_to_tokens",
        (tiles,),
        [pl.BlockSpec((rows, units), lambda i, r, s=s: (s, 0)) for s in range(2)]
        + [whole(g.shape) for g in grads]
        + [pl.BlockSpec((tile, w.shape[1]), lambda i, r: (side * tiles + i, 0)) for w in (up, qkv)],
        [pl.BlockSpec((rows, tile), lambda i, r: (0, i))] * 2,
        [((rows, features), BF16)] * 2,
        scratch=[
            pltpu.VMEM((2, rows, depth), BF16),
            pltpu.VMEM((tile, depth), BF16),
            pltpu.VMEM((rows, tile), BF16),
        ],
        prefetch=1,
        after=after,
    )(row, pre, pre, *grads, up, qkv)


def mix(row, places, count, sequence, hidden, attended, w_down, down_far, w_out, out_far, after=()):
    units, features = down_far.shape
    rows = hidden.shape[0] // 2
    heads = out_far.shape[0]
    tile = 2 * TILE
    tiles = features // tile
    depth = units + heads

    def kernel(row_ref, p_ref, h_ref, a_ref, dn_ref, df_ref, on_ref, of_ref, out_ref, x_ref, w_ref, scratch_ref):
        i = pl.program_id(0)

        @pl.when(i == 0)
        def _():
            x_ref[:, :units] = h_ref[...]
            x_ref[:, units:] = a_ref[...]

        @pl.when(i < tiles)
        def _():
            w_ref[:units] = dn_ref[...]
            w_ref[units:] = on_ref[...]

        @pl.when(i >= tiles)
        def _():
            w_ref[:units] = df_ref[...]
            w_ref[units:] = of_ref[...]

        write_blocks(row_ref, count, mul(x_ref[...], w_ref[...], NN), scratch_ref, out_ref)

    def near(height):
        return pl.BlockSpec((height, tile), lambda i, r, p: (2 * p[2] + p[0], jnp.minimum(i, tiles - 1)))

    def far(height):
        return pl.BlockSpec((height, tile), lambda i, r, p: (0, jnp.maximum(i - tiles, 0)))

    return call(
        kernel,
        "mix",
        (2 * tiles,),
        [pl.BlockSpec((rows, units), lambda i, r, p: (sequence, 0)), whole(attended.shape)]
        + [near(units), far(units), near(heads), far(heads)],
        [pl.BlockSpec((rows, tile), lambda i, r, p: (0, i))],
        [((rows, 2 * features), BF16)],
        scratch=[
            pltpu.VMEM((rows, depth), BF16),
            pltpu.VMEM((depth, tile), BF16),
            pltpu.VMEM((rows, tile), BF16),
        ],
        prefetch=2,
        after=after,
    )(row, places, hidden, attended, w_down, down_far, w_out, out_far)[0]


def add_blocks(kind, size, width, *terms, after=()):
    terms = [(*term, 0)[:3] for term in terms]

    def kernel(*refs):
        total = refs[0][...].astype(F32)
        for ref in refs[1:-1]:
            total = total + ref[...].astype(F32)
        refs[-1][...] = total.astype(kind)

    return call(
        kernel,
        "add_blocks",
        (1,),
        [pl.BlockSpec((size, width), lambda i, n=n, m=m: (n, m)) for _, n, m in terms],
        [whole((size, width))],
        [((size, width), kind)],
        after=after,
    )(*(array for array, _, _ in terms))[0]


def add_half(width, column, half, a, b, after=()):
    size = a.shape[0] // 4

    def kernel(a_ref, b_ref, out_ref):
        out_ref[...] = (a_ref[...].astype(F32) + b_ref[...].astype(F32)).astype(BF16)

    block = pl.BlockSpec((size, width), lambda i: (2 * half + i, column))
    return call(
        kernel,
        "add_half",
        (2,),
        [block, block],
        [pl.BlockSpec((size, width), lambda i: (i, 0))],
        [((2 * size, width), BF16)],
        after=after,
    )(a, b)[0]


def add_up(kind, *terms, after=()):
    def kernel(*refs):
        total = refs[0][...].astype(F32)
        for ref in refs[1:-1]:
            total = total + ref[...].astype(F32)
        refs[-1][...] = total.astype(kind)

    shape = terms[0].shape
    return call(
        kernel, "add_up", (1,), [whole(shape)] * len(terms), [whole(shape)], [(shape, kind)], after=after
    )(*terms)[0]


def add_pairs(kept, got, after=()):
    def kernel(near_ref, far_ref, got_ref, near_out, far_out):
        for i, (ref, out) in enumerate(((near_ref, near_out), (far_ref, far_out))):
            out[...] = (ref[...].astype(F32) + got_ref[i].astype(F32)).astype(BF16)

    shape = kept[0].shape
    return call(
        kernel,
        "add_pairs",
        (1,),
        [whole(shape), whole(shape), whole(got.shape)],
        [whole(shape)] * 2,
        [(shape, BF16)] * 2,
        after=after,
    )(*kept, got)


def rotary_rows(tokens):
    exponents = np.arange(0, ROT, 2).astype(np.float32) / np.float32(ROT)
    frequency = np.float32(10000.0) ** (-exponents)
    angles = (np.arange(tokens) % LEN).astype(np.float32)[:, None] * frequency[None, :]
    cosine, sine = np.cos(angles), np.sin(angles)
    none = np.zeros((tokens, ROT // 2), np.float32)
    rest = np.zeros((tokens, HEAD_DIM - ROT), np.float32)
    own = np.concatenate([cosine, cosine, rest + 1.0] * 2, axis=1)
    ahead = np.concatenate([-sine, none, rest] * 2, axis=1)
    behind = np.concatenate([none, sine, rest] * 2, axis=1)
    return tuple(table.astype(np.float32) for table in (own, ahead, behind))


def attention_kernel(
    sequence, places_ref, x_hbm, w_ref, bias_ref, near_ref, far_ref, on_ref, of_ref, own_ref, ahead_ref, behind_ref,
    *refs,
):
    *refs, x_ref, x_sem, q_ref, k_ref, v_ref, d_ref, dq_ref, dk_ref, dv_ref = refs
    got_ref = refs[0] if len(refs) == 7 else None
    out_ref, grad_ref, sum_ref, *weight_refs = refs if got_ref is None else refs[1:]
    half = ROT // 2
    rows, features = near_ref.shape
    own, ahead, behind = own_ref[...], ahead_ref[...], behind_ref[...]
    fetch = pltpu.make_async_copy(x_hbm.at[pl.ds(sequence * rows, rows)], x_ref, x_sem)
    fetch.start()

    def turn(x):
        return x * own + pltpu.roll(x, PAIR - half, 1) * ahead + pltpu.roll(x, half, 1) * behind

    def turn_back(x):
        return x * own - pltpu.roll(x, PAIR - half, 1) * ahead - pltpu.roll(x, half, 1) * behind

    grad_out = mul(near_ref[...], on_ref[...], NT) + mul(far_ref[...], of_ref[...], NT)
    grad_out = grad_out.astype(BF16)
    fetch.wait()
    pre = mul(x_ref[...], w_ref[...], NN) + bias_ref[...]
    biased = [pre[:, i * PAIR : (i + 1) * PAIR] for i in range(3)]
    query = turn(biased[0]).astype(BF16) * HEAD_DIM ** (-0.5)
    key = turn(biased[1]).astype(BF16)
    value = biased[2].astype(BF16)
    lane = lax.broadcasted_iota(jnp.int32, (rows, PAIR), 1)
    for head in range(2):
        mine = (lane >= head * HEAD_DIM) & (lane < (head + 1) * HEAD_DIM)
        for ref, array in ((q_ref, query), (k_ref, key), (v_ref, value), (d_ref, grad_out)):
            ref[head] = jnp.where(mine, array, jnp.zeros_like(array))

    tiles = rows // TILE
    for i in reversed(range(tiles)):
        at = pl.ds(i * TILE, TILE)
        span = (i + 1) * TILE
        attended = None
        grad_query = None
        for head in range(2):
            q, d = q_ref[head, at], d_ref[head, at]
            k, v = k_ref[head, :span], v_ref[head, :span]
            scores = mul(q, k, NT)
            row = lax.broadcasted_iota(jnp.int32, (TILE, span), 0) + i * TILE
            col = lax.broadcasted_iota(jnp.int32, (TILE, span), 1)
            scores = jnp.where(row >= col, scores, -1e30)
            e = jnp.exp(scores - jnp.max(scores, axis=1, keepdims=True))
            p = e * (1.0 / jnp.sum(e, axis=1, keepdims=True))
            w = p.astype(BF16)
            gw = mul(d, v, NT)
            gs = (p * (gw - jnp.sum(p * gw, axis=1, keepdims=True))).astype(BF16)
            o = mul(w, v, NN)
            gq = mul(gs, k, NN)
            attended = o if attended is None else attended + o
            grad_query = gq if grad_query is None else grad_query + gq
            gv = mul(w, d, TN)
            gk = mul(gs, q, TN)
            if i == tiles - 1 and head == 0:
                dv_ref[...] = gv
                dk_ref[...] = gk
            else:
                dv_ref[:span] += gv
                dk_ref[:span] += gk
        out_ref[at] = attended.astype(BF16)
        dq_ref[at] = grad_query
    gq = turn_back(dq_ref[...] * HEAD_DIM ** (-0.5)).astype(BF16)
    gk = turn_back(dk_ref[...]).astype(BF16)
    gv = dv_ref[...].astype(BF16)
    for i, g in enumerate((gq, gk, gv)):
        grad_ref[:, i * PAIR : (i + 1) * PAIR] = g
        sum_ref[:, i * PAIR : (i + 1) * PAIR] = jnp.sum(g.astype(F32), axis=0, keepdims=True)
    tile = 2 * features // 4
    for i in range(4):
        at = i * tile
        source = near_ref if at < features else far_ref
        block = jnp.concatenate(
            [
                mul(x_ref[:, at : at + tile], grad_ref[...], TN),
                mul(source[:, at % features : at % features + tile], out_ref[...], TN),
            ],
            axis=1,
        )
        if got_ref is None:
            weight_refs[0][at : at + tile] = block
        else:
            keep_tile(places_ref, i, block + got_ref[at : at + tile], *weight_refs)


def attention(places, sequence, x, qkv, bias, near, far, w_out, out_far, earlier=None, after=()):
    rows, features = near.shape
    wide = 3 * PAIR
    tables = [jnp.asarray(table) for table in rotary_rows(rows)]
    tile = 2 * features // 4
    earlier = [] if earlier is None else [earlier]
    if earlier:
        shapes = [((tile, 4 * PAIR), BF16)] * 2 + [((2, tile, 4 * PAIR), BF16)]
    else:
        shapes = [((4 * tile, 4 * PAIR), F32)]

    def kernel(*refs):
        attention_kernel(sequence, *refs)

    return call(
        kernel,
        "attention",
        (1,),
        [
            pl.BlockSpec(memory_space=pl.ANY),
            whole(qkv.shape),
            whole((1, wide)),
            whole(near.shape),
            whole(far.shape),
            pl.BlockSpec((PAIR, features), lambda i, p: (2 * p[2] + p[0], 0)),
            whole(out_far.shape),
        ]
        + [whole((rows, PAIR))] * 3
        + [whole(a.shape) for a in earlier],
        [whole((rows, PAIR)), whole((rows, wide)), whole((1, wide))] + [whole(shape) for shape, _ in shapes],
        [((rows, PAIR), BF16), ((rows, wide), BF16), ((1, wide), F32)] + shapes,
        scratch=[pltpu.VMEM((rows, 2 * features), BF16), pltpu.SemaphoreType.DMA]
        + [pltpu.VMEM((2, rows, PAIR), BF16)] * 4
        + [pltpu.VMEM((rows, PAIR), F32)] * 3,
        prefetch=1,
        after=after,
    )(places, x, qkv, bias.reshape(1, -1), near, far, w_out, out_far, *tables, *earlier)


def carry(array, after=()):
    def kernel(in_ref, out_ref):
        out_ref[...] = in_ref[...]

    half = pl.BlockSpec((array.shape[0] // 2, array.shape[1]), lambda i: (i, 0))
    return call(kernel, "carry", (2,), [half], [half], [(array.shape, array.dtype)], after=after)(array)[0]


def pair_up(first, second, after=()):
    shape = (2, *first.shape)

    def kernel(first_ref, second_ref, out_ref):
        for i, ref in enumerate((first_ref, second_ref)):

            @pl.when(pl.program_id(0) == i)
            def _(ref=ref):
                out_ref[0] = ref[...]

    return call(
        kernel,
        "pair_up",
        (2,),
        [whole(first.shape), whole(second.shape)],
        [pl.BlockSpec((1, *first.shape), lambda i: (i, 0, 0))],
        [(shape, first.dtype)],
        after=after,
    )(first, second)[0]


def place_kernel(places_ref, *refs):
    sources, targets = refs[:4], refs[4:]
    sibling, across, side = (pl.program_id(i) for i in range(3))
    for i in range(4):

        @pl.when((sibling == i // 2) & (across == i % 2))
        def _(source=sources[i]):
            block = source[side].astype(F32)
            if len(targets) == 1:
                targets[0][...] = block
            else:
                for t in range(3):
                    targets[t][...] = block[:, t * PAIR : (t + 1) * PAIR]
                targets[3][...] = block[:, 3 * PAIR :].T


def place(places, sources, blocks, shapes, maps, after=()):
    def spec(block, index):
        return pl.BlockSpec(block, lambda i, j, s, p: index(p[0] ^ i, p[1] ^ j, p[2] ^ s))

    return call(
        place_kernel,
        "place",
        (2, 2, 2),
        [whole(source.shape) for source in sources],
        [spec(*pair) for pair in zip(blocks, maps)],
        [(shape, F32) for shape in shapes],
        prefetch=1,
        after=after,
    )(places, *sources)


def swap(array, axis, bit=0, name="pieces"):
    size = lax.axis_size(axis)
    with jax.named_scope(name):
        return lax.ppermute(array, axis, [(i, i ^ (1 << bit)) for i in range(size)])


def step_up(array, name="row_ring"):
    size = lax.axis_size("row")
    with jax.named_scope(name):
        return lax.ppermute(array, "row", [(i, (i + 1) % size) for i in range(size)])


def part(array, index, parts, dim=0):
    size = array.shape[dim] // parts
    return lax.dynamic_slice_in_dim(array, index * size, size, dim)


def halves(array, dim):
    return jnp.split(array, 2, dim)


def pick(bit, first, second):
    return jnp.where(bit == 0, first, second)


def ordered(bit, mine, other, dim):
    return pick(bit, jnp.concatenate([mine, other], dim), jnp.concatenate([other, mine], dim))


def sync(*arrays):
    return lax.optimization_barrier(arrays)


def held(array, *others):
    return lax.optimization_barrier((array, *others))[0]


def add(a, b):
    return (a.astype(F32) + b.astype(F32)).astype(BF16)


def body(
    activations,
    ln_gain,
    ln_bias,
    w_query,
    w_key,
    w_value,
    b_query,
    b_key,
    b_value,
    w_out,
    w_up,
    b_up,
    w_down,
    out_bias,
    grad_out,
):
    dp, row, col = (lax.axis_index(axis) for axis in ("dp", "row", "col"))
    rows = lax.axis_size("row")
    bits = lax.axis_size("dp").bit_length() - 1
    places = [(dp >> bit) & 1 for bit in range(2)]
    where = jnp.stack([places[0], places[1], col]).astype(jnp.int32)
    here = row.reshape(1).astype(jnp.int32)
    own_rows, features = activations.shape
    feature_count = features * lax.axis_size("col")

    local = jnp.stack([jnp.sum(activations, axis=1), jnp.sum(activations * activations, axis=1)])
    early, third = cut_pieces(where, w_up, w_down, w_query, w_key, w_value, w_out)
    moments, early, third = sync(swap(local, "col"), early, third)
    moments = local + moments
    average = moments[0] / feature_count
    variance = moments[1] / feature_count - average * average
    inverse = lax.rsqrt(variance + 1e-05)[:, None]
    centered = (activations - average[:, None]) * inverse
    own = (centered * ln_gain + ln_bias).astype(BF16)

    def over_core(array, name="core"):
        return swap(array, "dp", 0, name)

    def over_x(array, name):
        return swap(array, "dp", 1, name)

    def over_col(array, name):
        return swap(array, "col", 0, name)

    biased = activations + out_bias

    near = [grad_out, over_core(grad_out, "grad_out")]
    own1 = step_up(own)
    other0 = over_col(own, "normed")
    early, other0 = sync(early, other0)
    early = over_col(early, "early")
    own2 = step_up(own1)
    front = jnp.concatenate([own, own1], 0)
    behind = jnp.concatenate([own2, other0], 0)
    ahead = step_up(behind)

    pieces = [early, over_x(early, "early")]
    up = join_up(where, w_up, pieces, after=near[1:])
    carried = carry(grad_out, after=[early])
    far = over_col(carried, "grad_out")
    other2 = step_up(take_half(ahead, after=[carried, up]))
    qkv, out_far = join_heads(where, w_query, w_key, w_value, pieces)
    third = over_col(third, "third")

    bias = [pick(places[0], *halves(b, 0)) for b in (b_query, b_key, b_value)]
    bias = jnp.concatenate(bias, 0)
    bias_up = pick(places[0], *halves(b_up, 0))

    front_sibling, behind_sibling, ahead_sibling = (
        over_core(a, "normed") for a in (front, behind, ahead)
    )
    blocks = [(front, 0), (behind, 1), (front_sibling, 0), (behind_sibling, 1)]
    blocks += [(front, 1), (ahead, 1), (front_sibling, 1), (ahead_sibling, 1)]
    normed, hidden, slope = hidden_units(
        here, rows, own_rows, range(2), blocks, up, bias_up, [], after=[qkv]
    )
    other2, hidden = sync(other2, hidden)
    other3 = step_up(other2)
    for step, mine, late in ((2, behind, other2), (3, ahead, other3)):
        sibling = behind_sibling if step == 2 else ahead_sibling
        blocks = [(mine, 0), (late, 0), (sibling, 0), (over_core(late, "normed"), 0)]
        normed, hidden, slope = hidden_units(
            here, rows, own_rows, range(step, step + 1), blocks, up, bias_up, [normed, hidden, slope]
        )

    def rest(total):
        for bit in range(2, bits):
            total = add(total, swap(total, "dp", bit))
        return total

    last = [hidden]

    def then(function, *arguments, pins=(), said=None):
        before = SAID[0]
        SAID[0] = before if said is None else said
        result = function(*arguments, after=[last[0], *pins])
        SAID[0] = before
        last[0] = jax.tree.leaves(result)[0]
        return result

    def plus(*terms, kind=BF16, pins=(), said=None):
        return then(
            lambda after: add_blocks(kind, own_rows, features, *terms, after=after), pins=pins, said=said
        )

    def plus_pairs(kept, got, pins=()):
        return [rest(total) for total in then(add_pairs, kept, got, pins=pins)]

    def attend(sequence, *arguments, pins=()):
        return then(
            lambda *a, after: attention(where, sequence, *a, after=after),
            normed, qkv, bias, near[sequence], far[sequence], w_out, out_far, *arguments, pins=pins,
        )

    def back(side, pins=()):
        return then(
            lambda *a, after: back_to_tokens(here, rows, side, *a, after=after),
            pre, qkv_grads, up, qkv, pins=pins,
        )

    def put(near, far, name, blocks, shapes, maps):
        pair = then(pair_up, near, far)
        across = over_x(pair, name)
        sources = [pair, across]

        def send():
            *sources[:], last[0] = sync(*sources, last[0])
            sources.extend(over_core(array, name) for array in sources[:])

        def write():
            return then(lambda *a, after: place(where, a, blocks, shapes, maps, after=after), *sources)

        return send, write, across

    def far_half(half, columns, own_terms, theirs, name):
        return over_col(
            then(lambda *a, after: add_half(features, columns, half, *a, after=after), own_terms, theirs), name
        )

    def outer_product(grads):
        return then(lambda *a, after: outer(where, *a, after=after), hidden, grads)

    far, last[0] = sync(far, last[0])
    far = [far, over_core(far, "grad_out")]
    attended0, grads0, sums0, weights = attend(0)
    third, last[0] = sync(third, last[0])
    third_across = over_x(third, "third")
    attended1, grads1, sums1, keep0, keep1, attn_send = attend(1, weights)
    attn_got = over_x(attn_send, "attn")
    qkv_grads = [grads0, grads1]

    down_far = then(lambda *a, after: join_down(where, *a, after=after), w_down, [third, third_across])

    def mixed_terms(sequence, attended):
        return then(
            lambda *a, after: mix(here, where, rows, sequence, *a, after=after),
            hidden, attended, w_down, down_far, w_out, out_far,
        )

    theirs = over_core(mixed_terms(1, attended1), "block_out")
    mixed = mixed_terms(0, attended0)
    out_first = far_half(0, 1, mixed, theirs, "block_out_col")

    pre, sum_up, up0, up1, up_send = then(
        lambda *a, after: hidden_back(where, *a, after=after), near, far, w_down, down_far, slope, normed
    )
    up_got = over_x(up_send, "up")
    attn_total = plus_pairs([keep0, keep1], attn_got)
    attn_mine = over_col(attn_total[1], "attn_far_col")

    near_terms, near_own = back(0)
    near_terms = over_core(near_terms, "grad_normed")
    far_terms, far_own = back(1)
    far_terms = over_core(far_terms, "grad_normed")
    mixed_next = step_up(
        plus((mixed, 0), (theirs, 0), (out_first, 0), pins=[attn_mine]), "block_out_ring"
    )
    SAID[0] = 1_300_000_000
    far_first = far_half(0, 0, far_own, far_terms, "grad_normed_col")

    near_keep, near_send = outer_product(near)
    near_got = over_x(near_send, "down_near")
    far_keep, far_send = outer_product(far)
    far_got = over_x(far_send, "down_far")

    up_total = plus_pairs([up0, up1], up_got, pins=[mixed_next])
    up_mine = over_col(up_total[1], "up_far_col")
    tall = attn_mine.shape[0]
    send_attn, put_attn, attn_across = put(
        attn_total[0], attn_mine,
        "attn_back",
        [(tall, PAIR)] * 3 + [(PAIR, tall)],
        [w_query.shape, w_key.shape, w_value.shape, w_out.shape],
        [lambda k, x, c: (x, c * 2 + k)] * 3 + [lambda k, x, c: (c * 2 + k, x)],
    )
    total = plus((near_own, 0), (near_terms, 0), (far_first, 0))
    total = step_up(total, "grad_normed_ring")
    far_second = far_half(1, 0, far_own, far_terms, "grad_normed_col")
    near_total = rest(plus((near_keep, 0), (near_got, 0)))
    far_total = rest(plus((far_keep, 0), (far_got, 0)))
    far_mine = over_col(far_total, "down_far_col")
    total = plus(
        (near_own, 1), (near_terms, 1), (far_first, 1), (total, 0), pins=[up_mine]
    )
    total = step_up(total, "grad_normed_ring")
    out_second = far_half(1, 1, mixed, theirs, "block_out_col")
    send_up, put_up, up_across = put(
        up_total[0], up_mine,
        "up_back",
        [up_mine.shape],
        [w_up.shape],
        [lambda k, x, c: (x, c * 2 + k)],
    )
    send_attn()
    total = plus((near_own, 2), (near_terms, 2), (far_second, 0), (total, 0), said=LARGE)
    total = step_up(total, "grad_normed_ring")
    mixed_next = step_up(plus((mixed, 1), (theirs, 1), (out_first, 1), (mixed_next, 0)), "block_out_ring")
    grad_w_query, grad_w_key, grad_w_value, grad_w_out = put_attn()
    send_down, put_down, down_across = put(
        near_total, far_mine,
        "down_back",
        [near_total.shape],
        [w_down.shape],
        [lambda k, x, c: (c * 4 + k * 2 + x, 0)],
    )
    send_up()
    grad_normed = plus(
        (near_own, 3), (near_terms, 3), (far_second, 1), (total, 0), kind=F32, said=LARGE
    )
    (grad_w_up,) = put_up()
    grad_normed, grad_w_up = sync(grad_normed, grad_w_up)
    mixed_next = step_up(
        plus((mixed, 2), (theirs, 2), (out_second, 0), (mixed_next, 0)), "block_out_ring"
    )
    send_down()
    (grad_w_down,) = put_down()
    block_out = plus(
        (mixed, 3), (theirs, 3), (out_second, 1), (mixed_next, 0), (biased, 0), kind=F32
    )
    SAID[0] = LARGE

    def over_all(array, axis, name):
        bits = lax.axis_size(axis).bit_length() - 1
        size = lax.axis_size(axis)
        for bit in range(0, bits, 2):
            masks = [1 << bit, 2 << bit, 3 << bit] if bit + 1 < bits else [1 << bit]
            with jax.named_scope(name):
                got = [lax.ppermute(array, axis, [(i, i ^ mask) for i in range(size)]) for mask in masks]
            array = array + got[0]
            if len(got) == 3:
                array = array + (got[1] + got[2])
        return array

    scaled = grad_normed * ln_gain
    local = jnp.stack([jnp.sum(scaled, axis=1), jnp.sum(scaled * centered, axis=1)])
    back_moments = (local + swap(local, "col", 0, "moments")) / feature_count
    own_grad = part(grad_out, row, rows).astype(F32)
    grad_activations = own_grad + inverse * (
        scaled - back_moments[0][:, None] - centered * back_moments[1][:, None]
    )
    grad_ln = jnp.stack([jnp.sum(grad_normed * centered, axis=0), jnp.sum(grad_normed, axis=0)])
    grad_ln = over_all(grad_ln, "row", "ln_row")

    sums = jnp.concatenate([sums0 + sums1, sum_up], 1)
    sums = ordered(places[0], sums, jnp.zeros_like(sums), 0)
    sizes = [grad_ln.size, sums.size]
    sums = jnp.concatenate([grad_ln.reshape(-1), sums.reshape(-1), jnp.sum(grad_out, axis=0, dtype=F32)])
    grad_ln, sums, grad_out_bias = jnp.split(over_all(sums, "dp", "sums"), [sizes[0], sum(sizes)])
    grad_ln, sums = grad_ln.reshape(2, -1), sums.reshape(2, -1)
    grad_bias = [sums[:, i * PAIR : (i + 1) * PAIR].reshape(-1) for i in range(3)]
    grad_b_up = sums[:, 3 * PAIR :].reshape(-1)


    return (
        block_out,
        grad_activations,
        grad_ln[0],
        grad_ln[1],
        grad_w_query,
        grad_w_key,
        grad_w_value,
        *grad_bias,
        grad_w_out,
        grad_w_up,
        grad_b_up,
        grad_w_down,
        grad_out_bias,
    )


def solution(mesh):
    placed = (
        P(("dp", "row"), "col"),
        P("col"),
        P("col"),
        P("col", "row"),
        P("col", "row"),
        P("col", "row"),
        P(("row", "col")),
        P(("row", "col")),
        P(("row", "col")),
        P("row", "col"),
        P("col", "row"),
        P(("row", "col")),
        P("row", "col"),
        P("col"),
        P("dp", "col"),
    )
    return jax.shard_map(
        body,
        mesh=mesh,
        in_specs=placed,
        out_specs=(
            P(("dp", "row"), "col"),
            P(("dp", "row"), "col"),
            P("col"),
            P("col"),
            P("col", "row"),
            P("col", "row"),
            P("col", "row"),
            P(("row", "col")),
            P(("row", "col")),
            P(("row", "col")),
            P("row", "col"),
            P("col", "row"),
            P(("row", "col")),
            P("row", "col"),
            P("col"),
        ),
        check_vma=False,
    )
```

```python
import jax
import jax.numpy as jnp
import numpy as np
from jax import lax
from jax.experimental import pallas as pl
from jax.experimental.pallas import tpu as pltpu
from jax.sharding import PartitionSpec as P

HEAD_DIM = 64
ROT = 32
LEN = 1024
BF16 = jnp.bfloat16
F32 = jnp.float32
TILE = 256
PAIR = 2 * HEAD_DIM
NN = (((1,), (0,)), ((), ()))
NT = (((1,), (1,)), ((), ()))
TN = (((0,), (0,)), ((), ()))
LARGE = 100_000_000_000
WORK = dict.fromkeys(("join_up", "join_heads", "hidden_units", "outer", "take_half", "carry"), 0)
SAID = [LARGE]


def mul(a, b, dims):
    return lax.dot_general(a, b, dims, preferred_element_type=F32)


def whole(shape):
    return pl.BlockSpec(shape, lambda *_: (0,) * len(shape))


def call(kernel, name, grid, in_specs, out_specs, out_shape, scratch=(), prefetch=0, vmem=60, after=(), aliases={}):
    given = prefetch + len(in_specs)

    def without(*refs):
        kernel(*refs[:given], *refs[given + len(after) :])

    function = pl.pallas_call(
        without,
        grid_spec=pltpu.PrefetchScalarGridSpec(
            num_scalar_prefetch=prefetch,
            grid=grid,
            in_specs=in_specs + [pl.BlockSpec(memory_space=pl.ANY)] * len(after),
            out_specs=out_specs,
            scratch_shapes=scratch,
        ),
        out_shape=[jax.ShapeDtypeStruct(*pair) for pair in out_shape],
        input_output_aliases=aliases,
        compiler_params=pltpu.CompilerParams(
            dimension_semantics=("arbitrary",) * len(grid), vmem_limit_bytes=vmem * 2**20
        ),
        cost_estimate=pl.CostEstimate(
            flops=WORK.get(name, SAID[0]), bytes_accessed=200_000_000, transcendentals=0
        ),
        name=name,
    )
    return lambda *arguments: function(*arguments, *after)


def cut_pieces(places, w_up, w_down, w_query, w_key, w_value, w_out):
    features = w_up.shape[0]
    rows = features // 2
    units = w_up.shape[1] // 4
    wide = 3 * PAIR
    height = PAIR // 2

    def kernel(p_ref, up_ref, down_ref, q_ref, k_ref, v_ref, out_ref, early_ref, third_ref):
        early_ref[:rows] = up_ref[...]
        third_ref[...] = down_ref[...]
        for i, ref in enumerate((q_ref, k_ref, v_ref)):
            early_ref[rows:, i * PAIR : (i + 1) * PAIR] = ref[...]
        for i in range(rows // height):
            at = rows + i * height
            early_ref[at : at + height, wide:] = out_ref[:, i * PAIR : (i + 1) * PAIR]

    def across(width):
        return pl.BlockSpec((rows, width), lambda i, p: (p[1], 2 * (1 - p[2]) + p[0]))

    def down(size):
        return pl.BlockSpec((size, features), lambda i, p: (4 * (1 - p[2]) + 2 * p[0] + p[1], 0))

    shapes = [(2 * rows, units), (units // 2, features)]
    return call(
        kernel,
        "cut_pieces",
        (1,),
        [across(units), down(units // 2), across(PAIR), across(PAIR), across(PAIR), down(height)],
        [whole(shape) for shape in shapes],
        [(shape, BF16) for shape in shapes],
        prefetch=1,
    )(places, w_up, w_down, w_query, w_key, w_value, w_out)


def at_half(places_ref, j, size):
    return pl.ds(pl.multiple_of((places_ref[1] ^ j) * size, size), size)


def join_up(places, w_up, pieces, after=()):
    features = w_up.shape[0]
    rows, units = pieces[0].shape[0] // 2, pieces[0].shape[1]

    def kernel(places_ref, near_ref, *refs):
        up_ref = refs[2]
        up_ref[:features] = near_ref[...]
        for j in range(2):
            up_ref[pl.ds(pl.multiple_of(features + (places_ref[1] ^ j) * rows, rows), rows), :] = refs[j][...]

    return call(
        kernel,
        "join_up",
        (1,),
        [pl.BlockSpec((features, units), lambda i, p: (0, 2 * p[2] + p[0]))]
        + [pl.BlockSpec((rows, units), lambda i, p: (0, 0))] * 2,
        [whole((2 * features, units))],
        [((2 * features, units), BF16)],
        prefetch=1,
        after=after,
    )(places, w_up, *pieces)[0]


def join_down(places, w_down, pieces, after=()):
    rows, features = pieces[0].shape

    def kernel(places_ref, *refs):
        for j in range(2):
            refs[2][at_half(places_ref, j, rows), :] = refs[j][...]

    return call(
        kernel,
        "join_down",
        (1,),
        [whole(a.shape) for a in pieces],
        [whole((2 * rows, features))],
        [((2 * rows, features), BF16)],
        prefetch=1,
        after=after,
    )(places, *pieces)[0]


def join_heads(places, w_query, w_key, w_value, pieces, after=()):
    features = w_query.shape[0]
    rows, width = pieces[0].shape[0] // 2, pieces[0].shape[1]
    wide = 3 * PAIR
    height = PAIR // 2

    def kernel(places_ref, q_ref, k_ref, v_ref, mine_ref, over_ref, qkv_ref, far_ref):
        for i, ref in enumerate((q_ref, k_ref, v_ref)):
            qkv_ref[:features, i * PAIR : (i + 1) * PAIR] = ref[...]

        def write(x):
            for j, ref in enumerate((mine_ref, over_ref)):
                at = x ^ j
                qkv_ref[features + at * rows : features + (at + 1) * rows, :] = ref[:, :wide]
                for i in range(rows // height):
                    far_ref[at * height : (at + 1) * height, i * PAIR : (i + 1) * PAIR] = ref[
                        i * height : (i + 1) * height, wide:
                    ]

        for x in range(2):
            pl.when(places_ref[1] == x)(lambda x=x: write(x))

    column = pl.BlockSpec((features, PAIR), lambda i, p: (0, 2 * p[2] + p[0]))
    shapes = [(2 * features, wide), (PAIR, features)]
    return call(
        kernel,
        "join_heads",
        (1,),
        [column, column, column] + [pl.BlockSpec((rows, width), lambda i, p: (1, 0))] * 2,
        [whole(shape) for shape in shapes],
        [(shape, BF16) for shape in shapes],
        prefetch=1,
        after=after,
    )(places, w_query, w_key, w_value, *pieces)


def token_block(row_ref, count, step):
    return lax.rem(row_ref[0] + 2 * count - step, count)


def hidden_units(row, count, size, steps, blocks, w, b, earlier, after=()):
    features = blocks[0][0].shape[1]
    depth, width = w.shape
    number = 2 * len(steps)

    def kernel(row_ref, *refs):
        x_refs, refs = refs[: 2 * number], refs[2 * number :]
        w_ref, b_ref, (x_ref, hidden_ref, slope_ref) = refs[0], refs[1], refs[-3:]
        for i in range(number):

            @pl.when(pl.program_id(0) == i)
            def _(i=i):
                x_ref[:, :features] = x_refs[2 * i][...]
                x_ref[:, features:] = x_refs[2 * i + 1][...]

        u = mul(x_ref[...], w_ref[...], NN) + b_ref[...]
        scale = (2.0 / np.pi) ** 0.5
        square = u * u
        t = jnp.tanh(scale * u * (1.0 + 0.044715 * square))
        half = 0.5 * (1.0 + t)
        hidden_ref[...] = (u * half).astype(BF16)
        slope_ref[...] = half + 0.5 * u * (1.0 - t * t) * scale * (1.0 + 3 * 0.044715 * square)

    def at(i, row_ref):
        return (i % 2 * count + token_block(row_ref, count, steps[0] + i // 2), 0)

    rows = 2 * count * size
    shapes = [((rows, depth), BF16), ((rows, width), BF16), ((rows, width), F32)]
    return call(
        kernel,
        "hidden_units",
        (number,),
        [pl.BlockSpec((size, features), lambda i, r, n=n: (n, 0)) for _, n in blocks]
        + [whole((depth, width)), whole((1, width))]
        + [pl.BlockSpec(memory_space=pl.ANY)] * len(earlier),
        [pl.BlockSpec((size, shape[1]), at) for shape, _ in shapes],
        shapes,
        prefetch=1,
        after=after,
        aliases={3 + len(blocks) + i: i for i in range(len(earlier))},
    )(row, *(array for array, _ in blocks), w, b.reshape(1, -1), *earlier)


def take_half(both, after=()):
    size, width = both.shape[0] // 2, both.shape[1]

    def kernel(in_ref, out_ref):
        out_ref[...] = in_ref[...]

    return call(
        kernel,
        "take_half",
        (1,),
        [pl.BlockSpec((size, width), lambda i: (1, 0))],
        [whole((size, width))],
        [((size, width), BF16)],
        after=after,
    )(both)[0]


def outer(places, a, grads, after=()):
    rows, width = grads[0].shape
    units = a.shape[1]
    half = units // 2

    def kernel(places_ref, a0_ref, a1_ref, b0_ref, b1_ref, kept_ref, sent_ref):
        total = (mul(a0_ref[...], b0_ref[...], TN) + mul(a1_ref[...], b1_ref[...], TN)).astype(BF16)
        for x in range(2):

            @pl.when(places_ref[1] == x)
            def _(x=x):
                kept_ref[...] = total[x * half : (x + 1) * half]
                sent_ref[...] = total[(1 - x) * half : (2 - x) * half]

    return call(
        kernel,
        "outer",
        (1,),
        [pl.BlockSpec((rows, units), lambda i, p, s=s: (s, 0)) for s in range(2)]
        + [whole((rows, width))] * 2,
        [whole((half, width))] * 2,
        [((half, width), BF16)] * 2,
        prefetch=1,
        after=after,
    )(places, a, a, *grads)


def keep_tile(places_ref, i, total, near_ref, far_ref, sent_ref):
    total = total.astype(BF16)

    @pl.when(places_ref[1] == i % 2)
    def _():
        (near_ref, far_ref)[i // 2][...] = total

    @pl.when(places_ref[1] != i % 2)
    def _():
        sent_ref[i // 2] = total


def hidden_back(places, near, far, w_down, w_far, slope, x, after=()):
    rows, features = near[0].shape
    units = w_far.shape[0]
    size = rows // 2
    steps = 2 * rows // size
    tile = x.shape[1] // 4

    def kernel(places_ref, n0, n1, f0, f1, wn_ref, wf_ref, slope_ref, x_hbm, pre_ref, sum_ref, *refs):
        outs, (x_ref, sem) = refs[:-2], refs[-2:]
        i = pl.program_id(0)
        fetch = pltpu.make_async_copy(x_hbm, x_ref, sem)

        @pl.when(i == 0)
        def _():
            fetch.start()
            sum_ref[...] = jnp.zeros_like(sum_ref)

        def write(near_ref, far_ref):
            g = mul(near_ref[...], wn_ref[...], NT) + mul(far_ref[...], wf_ref[...], NT)
            g = (g * slope_ref[...]).astype(BF16)
            pre_ref[pl.ds(pl.multiple_of(i * size, size), size), :] = g
            sum_ref[...] += jnp.sum(g.astype(F32), axis=0, keepdims=True)

        pl.when(i < steps // 2)(lambda: write(n0, f0))
        pl.when(i >= steps // 2)(lambda: write(n1, f1))

        @pl.when(i == steps - 1)
        def _():
            fetch.wait()
            for j in range(4):
                keep_tile(places_ref, j, mul(x_ref[:, j * tile : (j + 1) * tile], pre_ref[...], TN), *outs)

    first = pl.BlockSpec((size, features), lambda i, p: (jnp.minimum(i, steps // 2 - 1), 0))
    second = pl.BlockSpec((size, features), lambda i, p: (jnp.maximum(i - steps // 2, 0), 0))
    shapes = [(tile, units), (tile, units), (2, tile, units)]
    return call(
        kernel,
        "hidden_back",
        (steps,),
        [first, second, first, second]
        + [pl.BlockSpec((units, features), lambda i, p: (2 * p[2] + p[0], 0)), whole(w_far.shape)]
        + [pl.BlockSpec((size, units), lambda i, p: (i, 0)), pl.BlockSpec(memory_space=pl.ANY)],
        [whole((2 * rows, units)), whole((1, units))] + [whole(shape) for shape in shapes],
        [((2 * rows, units), BF16), ((1, units), F32)] + [(shape, BF16) for shape in shapes],
        scratch=[pltpu.VMEM(x.shape, BF16), pltpu.SemaphoreType.DMA],
        prefetch=1,
        after=after,
    )(places, *near, *far, w_down, w_far, slope, x)


def ring_order(row_ref, count, target, sources):
    size = target.shape[0] // count
    for i in range(count):
        at = pl.ds(pl.multiple_of(token_block(row_ref, count, 1 + i) * size, size), size)
        left = 0
        for source in sources:
            width = source.shape[1]
            target[i * size : (i + 1) * size, left : left + width] = source[at, :]
            left += width


def back_to_tokens(row, count, side, pre, grads, up, qkv, after=()):
    rows = grads[0].shape[0]
    features = up.shape[0] // 2
    units, wide = pre.shape[1], grads[0].shape[1]
    depth = units + wide
    tile = 2 * TILE
    tiles = features // tile

    def kernel(row_ref, p0, p1, g0, g1, up_ref, qkv_ref, theirs_ref, own_ref, x_ref, w_ref):
        w_ref[:, :units] = up_ref[...]
        w_ref[:, units:] = qkv_ref[...]
        for s, (p, g, out_ref) in enumerate(((p1, g1, theirs_ref), (p0, g0, own_ref))):

            @pl.when(pl.program_id(0) == 0)
            def _(s=s, p=p, g=g):
                ring_order(row_ref, count, x_ref.at[s], (p, g))

            out_ref[...] = mul(x_ref[s], w_ref[...], NT).astype(BF16)

    return call(
        kernel,
        "back_to_tokens",
        (tiles,),
        [pl.BlockSpec((rows, units), lambda i, r, s=s: (s, 0)) for s in range(2)]
        + [whole(g.shape) for g in grads]
        + [pl.BlockSpec((tile, w.shape[1]), lambda i, r: (side * tiles + i, 0)) for w in (up, qkv)],
        [pl.BlockSpec((rows, tile), lambda i, r: (0, i))] * 2,
        [((rows, features), BF16)] * 2,
        scratch=[
            pltpu.VMEM((2, rows, depth), BF16),
            pltpu.VMEM((tile, depth), BF16),
        ],
        prefetch=1,
        after=after,
    )(row, pre, pre, *grads, up, qkv)


def mix(row, places, count, sequence, hidden, attended, w_down, down_far, w_out, out_far, after=()):
    units, features = down_far.shape
    rows = hidden.shape[0] // 2
    heads = out_far.shape[0]
    tile = 2 * TILE
    tiles = features // tile
    depth = units + heads

    def kernel(row_ref, p_ref, h_ref, a_ref, dn_ref, df_ref, on_ref, of_ref, out_ref, x_ref, w_ref):
        i = pl.program_id(0)

        @pl.when(i == 0)
        def _():
            ring_order(row_ref, count, x_ref, (h_ref, a_ref))

        @pl.when(i < tiles)
        def _():
            w_ref[:units] = dn_ref[...]
            w_ref[units:] = on_ref[...]

        @pl.when(i >= tiles)
        def _():
            w_ref[:units] = df_ref[...]
            w_ref[units:] = of_ref[...]

        out_ref[...] = mul(x_ref[...], w_ref[...], NN).astype(BF16)

    def near(height):
        return pl.BlockSpec((height, tile), lambda i, r, p: (2 * p[2] + p[0], jnp.minimum(i, tiles - 1)))

    def far(height):
        return pl.BlockSpec((height, tile), lambda i, r, p: (0, jnp.maximum(i - tiles, 0)))

    return call(
        kernel,
        "mix",
        (2 * tiles,),
        [pl.BlockSpec((rows, units), lambda i, r, p: (sequence, 0)), whole(attended.shape)]
        + [near(units), far(units), near(heads), far(heads)],
        [pl.BlockSpec((rows, tile), lambda i, r, p: (0, i))],
        [((rows, 2 * features), BF16)],
        scratch=[
            pltpu.VMEM((rows, depth), BF16),
            pltpu.VMEM((depth, tile), BF16),
        ],
        prefetch=2,
        after=after,
    )(row, places, hidden, attended, w_down, down_far, w_out, out_far)[0]


def add_blocks(kind, size, width, *terms, after=()):
    terms = [(*term, 0)[:3] for term in terms]

    def kernel(*refs):
        total = refs[0][...].astype(F32)
        for ref in refs[1:-1]:
            total = total + ref[...].astype(F32)
        refs[-1][...] = total.astype(kind)

    return call(
        kernel,
        "add_blocks",
        (1,),
        [pl.BlockSpec((size, width), lambda i, n=n, m=m: (n, m)) for _, n, m in terms],
        [whole((size, width))],
        [((size, width), kind)],
        after=after,
    )(*(array for array, _, _ in terms))[0]


def add_half(width, column, half, a, b, after=()):
    size = a.shape[0] // 4

    def kernel(a_ref, b_ref, out_ref):
        out_ref[...] = (a_ref[...].astype(F32) + b_ref[...].astype(F32)).astype(BF16)

    block = pl.BlockSpec((size, width), lambda i: (2 * half + i, column))
    return call(
        kernel,
        "add_half",
        (2,),
        [block, block],
        [pl.BlockSpec((size, width), lambda i: (i, 0))],
        [((2 * size, width), BF16)],
        after=after,
    )(a, b)[0]


def add_up(kind, *terms, after=()):
    def kernel(*refs):
        total = refs[0][...].astype(F32)
        for ref in refs[1:-1]:
            total = total + ref[...].astype(F32)
        refs[-1][...] = total.astype(kind)

    shape = terms[0].shape
    return call(
        kernel, "add_up", (1,), [whole(shape)] * len(terms), [whole(shape)], [(shape, kind)], after=after
    )(*terms)[0]


def add_pairs(kept, got, after=()):
    def kernel(near_ref, far_ref, got_ref, near_out, far_out):
        for i, (ref, out) in enumerate(((near_ref, near_out), (far_ref, far_out))):
            out[...] = (ref[...].astype(F32) + got_ref[i].astype(F32)).astype(BF16)

    shape = kept[0].shape
    return call(
        kernel,
        "add_pairs",
        (1,),
        [whole(shape), whole(shape), whole(got.shape)],
        [whole(shape)] * 2,
        [(shape, BF16)] * 2,
        after=after,
    )(*kept, got)


def rotary_rows(tokens):
    exponents = np.arange(0, ROT, 2).astype(np.float32) / np.float32(ROT)
    frequency = np.float32(10000.0) ** (-exponents)
    angles = (np.arange(tokens) % LEN).astype(np.float32)[:, None] * frequency[None, :]
    cosine, sine = np.cos(angles), np.sin(angles)
    none = np.zeros((tokens, ROT // 2), np.float32)
    rest = np.zeros((tokens, HEAD_DIM - ROT), np.float32)
    own = np.concatenate([cosine, cosine, rest + 1.0] * 2, axis=1)
    ahead = np.concatenate([-sine, none, rest] * 2, axis=1)
    behind = np.concatenate([none, sine, rest] * 2, axis=1)
    return tuple(table.astype(np.float32) for table in (own, ahead, behind))


def attention_kernel(
    sequence, places_ref, x_hbm, w_ref, bias_ref, near_hbm, far_hbm, on_ref, of_ref, own_ref, ahead_ref, behind_ref,
    *refs,
):
    *refs, x_ref, near_ref, far_ref, got_ref, sems, q_ref, k_ref, v_ref, d_ref, dq_ref, dk_ref, dv_ref = refs
    got_hbm = refs[0] if len(refs) == 7 else None
    out_ref, grad_ref, sum_ref, *weight_refs = refs if got_hbm is None else refs[1:]
    half = ROT // 2
    rows, features = near_hbm.shape
    own, ahead, behind = own_ref[...], ahead_ref[...], behind_ref[...]
    copies = [
        pltpu.make_async_copy(x_hbm.at[pl.ds(sequence * rows, rows)], x_ref, sems.at[0]),
        pltpu.make_async_copy(near_hbm, near_ref, sems.at[1]),
        pltpu.make_async_copy(far_hbm, far_ref, sems.at[2]),
    ]
    if got_hbm is not None:
        copies.append(pltpu.make_async_copy(got_hbm, got_ref, sems.at[3]))
    for copy in copies:
        copy.start()

    def turn(x):
        return x * own + pltpu.roll(x, PAIR - half, 1) * ahead + pltpu.roll(x, half, 1) * behind

    def turn_back(x):
        return x * own - pltpu.roll(x, PAIR - half, 1) * ahead - pltpu.roll(x, half, 1) * behind

    copies[0].wait()
    pre = mul(x_ref[...], w_ref[...], NN) + bias_ref[...]
    copies[1].wait()
    copies[2].wait()
    grad_out = mul(near_ref[...], on_ref[...], NT) + mul(far_ref[...], of_ref[...], NT)
    grad_out = grad_out.astype(BF16)
    biased = [pre[:, i * PAIR : (i + 1) * PAIR] for i in range(3)]
    query = turn(biased[0]).astype(BF16) * HEAD_DIM ** (-0.5)
    key = turn(biased[1]).astype(BF16)
    value = biased[2].astype(BF16)
    lane = lax.broadcasted_iota(jnp.int32, (rows, PAIR), 1)
    for head in range(2):
        mine = (lane >= head * HEAD_DIM) & (lane < (head + 1) * HEAD_DIM)
        for ref, array in ((q_ref, query), (k_ref, key), (v_ref, value), (d_ref, grad_out)):
            ref[head] = jnp.where(mine, array, jnp.zeros_like(array))

    tiles = rows // TILE
    for i in reversed(range(tiles)):
        at = pl.ds(i * TILE, TILE)
        span = (i + 1) * TILE
        attended = None
        grad_query = None
        for head in range(2):
            q, d = q_ref[head, at], d_ref[head, at]
            k, v = k_ref[head, :span], v_ref[head, :span]
            scores = mul(q, k, NT)
            row = lax.broadcasted_iota(jnp.int32, (TILE, span), 0) + i * TILE
            col = lax.broadcasted_iota(jnp.int32, (TILE, span), 1)
            scores = jnp.where(row >= col, scores, -1e30)
            e = jnp.exp(scores - jnp.max(scores, axis=1, keepdims=True))
            p = e * (1.0 / jnp.sum(e, axis=1, keepdims=True))
            w = p.astype(BF16)
            gw = mul(d, v, NT)
            gs = (p * (gw - jnp.sum(p * gw, axis=1, keepdims=True))).astype(BF16)
            o = mul(w, v, NN)
            gq = mul(gs, k, NN)
            attended = o if attended is None else attended + o
            grad_query = gq if grad_query is None else grad_query + gq
            gv = mul(w, d, TN)
            gk = mul(gs, q, TN)
            if i == tiles - 1 and head == 0:
                dv_ref[...] = gv
                dk_ref[...] = gk
            else:
                dv_ref[:span] += gv
                dk_ref[:span] += gk
        out_ref[at] = attended.astype(BF16)
        dq_ref[at] = grad_query
    gq = turn_back(dq_ref[...] * HEAD_DIM ** (-0.5)).astype(BF16)
    gk = turn_back(dk_ref[...]).astype(BF16)
    gv = dv_ref[...].astype(BF16)
    for i, g in enumerate((gq, gk, gv)):
        grad_ref[:, i * PAIR : (i + 1) * PAIR] = g
        sum_ref[:, i * PAIR : (i + 1) * PAIR] = jnp.sum(g.astype(F32), axis=0, keepdims=True)
    if got_hbm is not None:
        copies[3].wait()
    tile = 2 * features // 4
    for i in range(4):
        at = i * tile
        source = near_ref if at < features else far_ref
        block = jnp.concatenate(
            [
                mul(x_ref[:, at : at + tile], grad_ref[...], TN),
                mul(source[:, at % features : at % features + tile], out_ref[...], TN),
            ],
            axis=1,
        )
        if got_hbm is None:
            weight_refs[0][at : at + tile] = block.astype(BF16)
        else:
            keep_tile(places_ref, i, block + got_ref[at : at + tile].astype(F32), *weight_refs)


def attention(places, sequence, x, qkv, bias, near, far, w_out, out_far, earlier=None, after=()):
    rows, features = near.shape
    wide = 3 * PAIR
    tables = [jnp.asarray(table) for table in rotary_rows(rows)]
    tile = 2 * features // 4
    earlier = [] if earlier is None else [earlier]
    if earlier:
        shapes = [((tile, 4 * PAIR), BF16)] * 2 + [((2, tile, 4 * PAIR), BF16)]
    else:
        shapes = [((4 * tile, 4 * PAIR), BF16)]

    def kernel(*refs):
        attention_kernel(sequence, *refs)

    return call(
        kernel,
        "attention",
        (1,),
        [
            pl.BlockSpec(memory_space=pl.ANY),
            whole(qkv.shape),
            whole((1, wide)),
            pl.BlockSpec(memory_space=pl.ANY),
            pl.BlockSpec(memory_space=pl.ANY),
            pl.BlockSpec((PAIR, features), lambda i, p: (2 * p[2] + p[0], 0)),
            whole(out_far.shape),
        ]
        + [whole((rows, PAIR))] * 3
        + [pl.BlockSpec(memory_space=pl.ANY)] * len(earlier),
        [whole((rows, PAIR)), whole((rows, wide)), whole((1, wide))] + [whole(shape) for shape, _ in shapes],
        [((rows, PAIR), BF16), ((rows, wide), BF16), ((1, wide), F32)] + shapes,
        scratch=[pltpu.VMEM((rows, 2 * features), BF16)]
        + [pltpu.VMEM((rows, features), BF16)] * 2
        + [pltpu.VMEM((4 * tile, 4 * PAIR), BF16), pltpu.SemaphoreType.DMA((4,))]
        + [pltpu.VMEM((2, rows, PAIR), BF16)] * 4
        + [pltpu.VMEM((rows, PAIR), F32)] * 3,
        prefetch=1,
        after=after,
    )(places, x, qkv, bias.reshape(1, -1), near, far, w_out, out_far, *tables, *earlier)


def carry(array, after=()):
    def kernel(in_ref, out_ref):
        out_ref[...] = in_ref[...]

    half = pl.BlockSpec((array.shape[0] // 2, array.shape[1]), lambda i: (i, 0))
    return call(kernel, "carry", (2,), [half], [half], [(array.shape, array.dtype)], after=after)(array)[0]


def pair_up(first, second, after=()):
    shape = (2, *first.shape)

    def kernel(first_ref, second_ref, out_ref):
        for i, ref in enumerate((first_ref, second_ref)):

            @pl.when(pl.program_id(0) == i)
            def _(ref=ref):
                out_ref[0] = ref[...]

    return call(
        kernel,
        "pair_up",
        (2,),
        [whole(first.shape), whole(second.shape)],
        [pl.BlockSpec((1, *first.shape), lambda i: (i, 0, 0))],
        [(shape, first.dtype)],
        after=after,
    )(first, second)[0]


def place_kernel(places_ref, *refs):
    sources, targets = refs[:4], refs[4:]
    sibling, across, side = (pl.program_id(i) for i in range(3))
    for i in range(4):

        @pl.when((sibling == i // 2) & (across == i % 2))
        def _(source=sources[i]):
            block = source[side].astype(F32)
            if len(targets) == 1:
                targets[0][...] = block
            else:
                for t in range(3):
                    targets[t][...] = block[:, t * PAIR : (t + 1) * PAIR]
                targets[3][...] = block[:, 3 * PAIR :].T


def place(places, sources, blocks, shapes, maps, after=()):
    def spec(block, index):
        return pl.BlockSpec(block, lambda i, j, s, p: index(p[0] ^ i, p[1] ^ j, p[2] ^ s))

    return call(
        place_kernel,
        "place",
        (2, 2, 2),
        [whole(source.shape) for source in sources],
        [spec(*pair) for pair in zip(blocks, maps)],
        [(shape, F32) for shape in shapes],
        prefetch=1,
        after=after,
    )(places, *sources)


def swap(array, axis, bit=0, name="pieces"):
    size = lax.axis_size(axis)
    with jax.named_scope(name):
        return lax.ppermute(array, axis, [(i, i ^ (1 << bit)) for i in range(size)])


def step_up(array, name="row_ring"):
    size = lax.axis_size("row")
    with jax.named_scope(name):
        return lax.ppermute(array, "row", [(i, (i + 1) % size) for i in range(size)])


def part(array, index, parts, dim=0):
    size = array.shape[dim] // parts
    return lax.dynamic_slice_in_dim(array, index * size, size, dim)


def halves(array, dim):
    return jnp.split(array, 2, dim)


def pick(bit, first, second):
    return jnp.where(bit == 0, first, second)


def ordered(bit, mine, other, dim):
    return pick(bit, jnp.concatenate([mine, other], dim), jnp.concatenate([other, mine], dim))


def sync(*arrays):
    return lax.optimization_barrier(arrays)


def held(array, *others):
    return lax.optimization_barrier((array, *others))[0]


def add(a, b):
    return (a.astype(F32) + b.astype(F32)).astype(BF16)


def body(
    activations,
    ln_gain,
    ln_bias,
    w_query,
    w_key,
    w_value,
    b_query,
    b_key,
    b_value,
    w_out,
    w_up,
    b_up,
    w_down,
    out_bias,
    grad_out,
):
    dp, row, col = (lax.axis_index(axis) for axis in ("dp", "row", "col"))
    rows = lax.axis_size("row")
    bits = lax.axis_size("dp").bit_length() - 1
    places = [(dp >> bit) & 1 for bit in range(2)]
    where = jnp.stack([places[0], places[1], col]).astype(jnp.int32)
    here = row.reshape(1).astype(jnp.int32)
    own_rows, features = activations.shape
    feature_count = features * lax.axis_size("col")

    local = jnp.stack([jnp.sum(activations, axis=1), jnp.sum(activations * activations, axis=1)])
    early, third = cut_pieces(where, w_up, w_down, w_query, w_key, w_value, w_out)
    moments, early, third = sync(swap(local, "col"), early, third)
    moments = local + moments
    average = moments[0] / feature_count
    variance = moments[1] / feature_count - average * average
    inverse = lax.rsqrt(variance + 1e-05)[:, None]
    centered = (activations - average[:, None]) * inverse
    own = (centered * ln_gain + ln_bias).astype(BF16)

    def over_core(array, name="core"):
        return swap(array, "dp", 0, name)

    def over_x(array, name):
        return swap(array, "dp", 1, name)

    def over_col(array, name):
        return swap(array, "col", 0, name)

    biased = activations + out_bias

    near = [grad_out, over_core(grad_out, "grad_out")]
    own1 = step_up(own)
    other0 = over_col(own, "normed")
    early, other0 = sync(early, other0)
    early = over_col(early, "early")
    own2 = step_up(own1)
    front = jnp.concatenate([own, own1], 0)
    behind = jnp.concatenate([own2, other0], 0)
    ahead = step_up(behind)

    pieces = [early, over_x(early, "early")]
    up = join_up(where, w_up, pieces, after=near[1:])
    carried = carry(grad_out, after=[early])
    far = over_col(carried, "grad_out")
    other2 = step_up(take_half(ahead, after=[carried]))
    qkv, out_far = join_heads(where, w_query, w_key, w_value, pieces)
    third = over_col(third, "third")

    bias = [pick(places[0], *halves(b, 0)) for b in (b_query, b_key, b_value)]
    bias = jnp.concatenate(bias, 0)
    bias_up = pick(places[0], *halves(b_up, 0))

    front_sibling, behind_sibling, ahead_sibling = (
        over_core(a, "normed") for a in (front, behind, ahead)
    )
    blocks = [(front, 0), (behind, 1), (front_sibling, 0), (behind_sibling, 1)]
    blocks += [(front, 1), (ahead, 1), (front_sibling, 1), (ahead_sibling, 1)]
    normed, hidden, slope = hidden_units(
        here, rows, own_rows, range(2), blocks, up, bias_up, []
    )
    other2, hidden, qkv = sync(other2, hidden, qkv)
    other3 = step_up(other2)
    for step, mine, late in ((2, behind, other2), (3, ahead, other3)):
        sibling = behind_sibling if step == 2 else ahead_sibling
        blocks = [(mine, 0), (late, 0), (sibling, 0), (over_core(late, "normed"), 0)]
        normed, hidden, slope = hidden_units(
            here, rows, own_rows, range(step, step + 1), blocks, up, bias_up, [normed, hidden, slope]
        )

    def rest(total):
        for bit in range(2, bits):
            total = add(total, swap(total, "dp", bit))
        return total

    last = [hidden]

    def then(function, *arguments, pins=(), said=None):
        before = SAID[0]
        SAID[0] = before if said is None else said
        result = function(*arguments, after=[last[0], *pins])
        SAID[0] = before
        last[0] = jax.tree.leaves(result)[0]
        return result

    def plus(*terms, kind=BF16, pins=(), said=None):
        return then(
            lambda after: add_blocks(kind, own_rows, features, *terms, after=after), pins=pins, said=said
        )

    def plus_pairs(kept, got, pins=()):
        return [rest(total) for total in then(add_pairs, kept, got, pins=pins)]

    def attend(sequence, *arguments, pins=()):
        return then(
            lambda *a, after: attention(where, sequence, *a, after=after),
            normed, qkv, bias, near[sequence], far[sequence], w_out, out_far, *arguments, pins=pins,
        )

    def back(side, pins=()):
        return then(
            lambda *a, after: back_to_tokens(here, rows, side, *a, after=after),
            pre, qkv_grads, up, qkv, pins=pins,
        )

    def put(near, far, name, blocks, shapes, maps):
        pair = then(pair_up, near, far)
        across = over_x(pair, name)
        sources = [pair, across]

        def send():
            *sources[:], last[0] = sync(*sources, last[0])
            sources.extend(over_core(array, name) for array in sources[:])

        def write():
            return then(lambda *a, after: place(where, a, blocks, shapes, maps, after=after), *sources)

        return send, write, across

    def far_half(half, columns, own_terms, theirs, name):
        return over_col(
            then(lambda *a, after: add_half(features, columns, half, *a, after=after), own_terms, theirs), name
        )

    def outer_product(grads):
        return then(lambda *a, after: outer(where, *a, after=after), hidden, grads)

    far, last[0] = sync(far, last[0])
    far = [far, over_core(far, "grad_out")]
    attended0, grads0, sums0, weights = attend(0)
    third, last[0] = sync(third, last[0])
    third_across = over_x(third, "third")
    attended1, grads1, sums1, keep0, keep1, attn_send = attend(1, weights)
    attn_got = over_x(attn_send, "attn")
    qkv_grads = [grads0, grads1]

    down_far = then(lambda *a, after: join_down(where, *a, after=after), w_down, [third, third_across])

    def mixed_terms(sequence, attended):
        return then(
            lambda *a, after: mix(here, where, rows, sequence, *a, after=after),
            hidden, attended, w_down, down_far, w_out, out_far,
        )

    theirs = over_core(mixed_terms(1, attended1), "block_out")
    mixed = mixed_terms(0, attended0)
    out_first = far_half(0, 1, mixed, theirs, "block_out_col")

    pre, sum_up, up0, up1, up_send = then(
        lambda *a, after: hidden_back(where, *a, after=after), near, far, w_down, down_far, slope, normed
    )
    up_got = over_x(up_send, "up")
    attn_total = plus_pairs([keep0, keep1], attn_got)
    attn_mine = over_col(attn_total[1], "attn_far_col")

    near_terms, near_own = back(0)
    near_terms = over_core(near_terms, "grad_normed")
    far_terms, far_own = back(1)
    far_terms = over_core(far_terms, "grad_normed")
    mixed_next = step_up(
        plus((mixed, 0), (theirs, 0), (out_first, 0), pins=[attn_mine]), "block_out_ring"
    )
    SAID[0] = 1_300_000_000
    far_first = far_half(0, 0, far_own, far_terms, "grad_normed_col")

    near_keep, near_send = outer_product(near)
    near_got = over_x(near_send, "down_near")
    far_keep, far_send = outer_product(far)
    far_got = over_x(far_send, "down_far")

    up_total = plus_pairs([up0, up1], up_got, pins=[mixed_next])
    up_mine = over_col(up_total[1], "up_far_col")
    tall = attn_mine.shape[0]
    send_attn, put_attn, attn_across = put(
        attn_total[0], attn_mine,
        "attn_back",
        [(tall, PAIR)] * 3 + [(PAIR, tall)],
        [w_query.shape, w_key.shape, w_value.shape, w_out.shape],
        [lambda k, x, c: (x, c * 2 + k)] * 3 + [lambda k, x, c: (c * 2 + k, x)],
    )
    total = plus((near_own, 0), (near_terms, 0), (far_first, 0))
    total = step_up(total, "grad_normed_ring")
    far_second = far_half(1, 0, far_own, far_terms, "grad_normed_col")
    near_total = rest(plus((near_keep, 0), (near_got, 0)))
    far_total = rest(plus((far_keep, 0), (far_got, 0)))
    far_mine = over_col(far_total, "down_far_col")
    total = plus(
        (near_own, 1), (near_terms, 1), (far_first, 1), (total, 0), pins=[up_mine]
    )
    total = step_up(total, "grad_normed_ring")
    out_second = far_half(1, 1, mixed, theirs, "block_out_col")
    send_up, put_up, up_across = put(
        up_total[0], up_mine,
        "up_back",
        [up_mine.shape],
        [w_up.shape],
        [lambda k, x, c: (x, c * 2 + k)],
    )
    send_attn()
    total = plus((near_own, 2), (near_terms, 2), (far_second, 0), (total, 0), said=LARGE)
    total = step_up(total, "grad_normed_ring")
    mixed_next = step_up(plus((mixed, 1), (theirs, 1), (out_first, 1), (mixed_next, 0)), "block_out_ring")
    grad_w_query, grad_w_key, grad_w_value, grad_w_out = put_attn()
    send_down, put_down, down_across = put(
        near_total, far_mine,
        "down_back",
        [near_total.shape],
        [w_down.shape],
        [lambda k, x, c: (c * 4 + k * 2 + x, 0)],
    )
    send_up()
    grad_normed = plus(
        (near_own, 3), (near_terms, 3), (far_second, 1), (total, 0), kind=F32, said=LARGE
    )
    (grad_w_up,) = put_up()
    grad_normed, grad_w_up = sync(grad_normed, grad_w_up)
    mixed_next = step_up(
        plus((mixed, 2), (theirs, 2), (out_second, 0), (mixed_next, 0)), "block_out_ring"
    )
    send_down()
    (grad_w_down,) = put_down()
    block_out = plus(
        (mixed, 3), (theirs, 3), (out_second, 1), (mixed_next, 0), (biased, 0), kind=F32
    )
    SAID[0] = LARGE

    def over_all(array, axis, name):
        bits = lax.axis_size(axis).bit_length() - 1
        size = lax.axis_size(axis)
        for bit in range(0, bits, 2):
            masks = [1 << bit, 2 << bit, 3 << bit] if bit + 1 < bits else [1 << bit]
            with jax.named_scope(name):
                got = [lax.ppermute(array, axis, [(i, i ^ mask) for i in range(size)]) for mask in masks]
            array = array + got[0]
            if len(got) == 3:
                array = array + (got[1] + got[2])
        return array

    scaled = grad_normed * ln_gain
    local = jnp.stack([jnp.sum(scaled, axis=1), jnp.sum(scaled * centered, axis=1)])
    back_moments = (local + swap(local, "col", 0, "moments")) / feature_count
    own_grad = part(grad_out, row, rows).astype(F32)
    grad_activations = own_grad + inverse * (
        scaled - back_moments[0][:, None] - centered * back_moments[1][:, None]
    )
    grad_ln = jnp.stack([jnp.sum(grad_normed * centered, axis=0), jnp.sum(grad_normed, axis=0)])
    grad_ln = over_all(grad_ln, "row", "ln_row")

    sums = jnp.concatenate([sums0 + sums1, sum_up], 1)
    sums = ordered(places[0], sums, jnp.zeros_like(sums), 0)
    sizes = [grad_ln.size, sums.size]
    sums = jnp.concatenate([grad_ln.reshape(-1), sums.reshape(-1), jnp.sum(grad_out, axis=0, dtype=F32)])
    grad_ln, sums, grad_out_bias = jnp.split(over_all(sums, "dp", "sums"), [sizes[0], sum(sizes)])
    grad_ln, sums = grad_ln.reshape(2, -1), sums.reshape(2, -1)
    grad_bias = [sums[:, i * PAIR : (i + 1) * PAIR].reshape(-1) for i in range(3)]
    grad_b_up = sums[:, 3 * PAIR :].reshape(-1)


    return (
        block_out,
        grad_activations,
        grad_ln[0],
        grad_ln[1],
        grad_w_query,
        grad_w_key,
        grad_w_value,
        *grad_bias,
        grad_w_out,
        grad_w_up,
        grad_b_up,
        grad_w_down,
        grad_out_bias,
    )


def solution(mesh):
    placed = (
        P(("dp", "row"), "col"),
        P("col"),
        P("col"),
        P("col", "row"),
        P("col", "row"),
        P("col", "row"),
        P(("row", "col")),
        P(("row", "col")),
        P(("row", "col")),
        P("row", "col"),
        P("col", "row"),
        P(("row", "col")),
        P("row", "col"),
        P("col"),
        P("dp", "col"),
    )
    return jax.shard_map(
        body,
        mesh=mesh,
        in_specs=placed,
        out_specs=(
            P(("dp", "row"), "col"),
            P(("dp", "row"), "col"),
            P("col"),
            P("col"),
            P("col", "row"),
            P("col", "row"),
            P("col", "row"),
            P(("row", "col")),
            P(("row", "col")),
            P(("row", "col")),
            P("row", "col"),
            P("col", "row"),
            P(("row", "col")),
            P("row", "col"),
            P("col"),
        ),
        check_vma=False,
    )
```

```python
import jax
import jax.numpy as jnp
import numpy as np
from jax import lax
from jax.experimental import pallas as pl
from jax.experimental.pallas import tpu as pltpu
from jax.sharding import PartitionSpec as P

HEAD_DIM = 64
ROT = 32
LEN = 1024
BF16 = jnp.bfloat16
F32 = jnp.float32
TILE = 256
PAIR = 2 * HEAD_DIM
NN = (((1,), (0,)), ((), ()))
NT = (((1,), (1,)), ((), ()))
TN = (((0,), (0,)), ((), ()))
LARGE = 100_000_000_000
WORK = dict.fromkeys(("join_up", "join_heads", "hidden_units", "outer", "take_half", "carry"), 0)
SAID = [LARGE]


def mul(a, b, dims):
    return lax.dot_general(a, b, dims, preferred_element_type=F32)


def whole(shape):
    return pl.BlockSpec(shape, lambda *_: (0,) * len(shape))


def call(kernel, name, grid, in_specs, out_specs, out_shape, scratch=(), prefetch=0, vmem=60, after=(), aliases={}):
    given = prefetch + len(in_specs)

    def without(*refs):
        kernel(*refs[:given], *refs[given + len(after) :])

    function = pl.pallas_call(
        without,
        grid_spec=pltpu.PrefetchScalarGridSpec(
            num_scalar_prefetch=prefetch,
            grid=grid,
            in_specs=in_specs + [pl.BlockSpec(memory_space=pl.ANY)] * len(after),
            out_specs=out_specs,
            scratch_shapes=scratch,
        ),
        out_shape=[jax.ShapeDtypeStruct(*pair) for pair in out_shape],
        input_output_aliases=aliases,
        compiler_params=pltpu.CompilerParams(
            dimension_semantics=("arbitrary",) * len(grid), vmem_limit_bytes=vmem * 2**20
        ),
        cost_estimate=pl.CostEstimate(
            flops=WORK.get(name, SAID[0]), bytes_accessed=200_000_000, transcendentals=0
        ),
        name=name,
    )
    return lambda *arguments: function(*arguments, *after)


def cut_pieces(places, w_up, w_down, w_query, w_key, w_value, w_out):
    features = w_up.shape[0]
    rows = features // 2
    units = w_up.shape[1] // 4
    wide = 3 * PAIR
    height = PAIR // 2

    def kernel(p_ref, up_ref, down_ref, q_ref, k_ref, v_ref, out_ref, early_ref, third_ref):
        early_ref[:rows] = up_ref[...]
        third_ref[...] = down_ref[...]
        for i, ref in enumerate((q_ref, k_ref, v_ref)):
            early_ref[rows:, i * PAIR : (i + 1) * PAIR] = ref[...]
        for i in range(rows // height):
            at = rows + i * height
            early_ref[at : at + height, wide:] = out_ref[:, i * PAIR : (i + 1) * PAIR]

    def across(width):
        return pl.BlockSpec((rows, width), lambda i, p: (p[1], 2 * (1 - p[2]) + p[0]))

    def down(size):
        return pl.BlockSpec((size, features), lambda i, p: (4 * (1 - p[2]) + 2 * p[0] + p[1], 0))

    shapes = [(2 * rows, units), (units // 2, features)]
    return call(
        kernel,
        "cut_pieces",
        (1,),
        [across(units), down(units // 2), across(PAIR), across(PAIR), across(PAIR), down(height)],
        [whole(shape) for shape in shapes],
        [(shape, BF16) for shape in shapes],
        prefetch=1,
    )(places, w_up, w_down, w_query, w_key, w_value, w_out)


def at_half(places_ref, j, size):
    return pl.ds(pl.multiple_of((places_ref[1] ^ j) * size, size), size)


def join_up(places, w_up, pieces, after=()):
    features = w_up.shape[0]
    rows, units = pieces[0].shape[0] // 2, pieces[0].shape[1]

    def kernel(places_ref, near_ref, *refs):
        up_ref = refs[2]
        up_ref[:features] = near_ref[...]
        for j in range(2):
            up_ref[pl.ds(pl.multiple_of(features + (places_ref[1] ^ j) * rows, rows), rows), :] = refs[j][...]

    return call(
        kernel,
        "join_up",
        (1,),
        [pl.BlockSpec((features, units), lambda i, p: (0, 2 * p[2] + p[0]))]
        + [pl.BlockSpec((rows, units), lambda i, p: (0, 0))] * 2,
        [whole((2 * features, units))],
        [((2 * features, units), BF16)],
        prefetch=1,
        after=after,
    )(places, w_up, *pieces)[0]


def join_down(places, w_down, pieces, after=()):
    rows, features = pieces[0].shape

    def kernel(places_ref, *refs):
        for j in range(2):
            refs[2][at_half(places_ref, j, rows), :] = refs[j][...]

    return call(
        kernel,
        "join_down",
        (1,),
        [whole(a.shape) for a in pieces],
        [whole((2 * rows, features))],
        [((2 * rows, features), BF16)],
        prefetch=1,
        after=after,
    )(places, *pieces)[0]


def join_heads(places, w_query, w_key, w_value, pieces, after=()):
    features = w_query.shape[0]
    rows, width = pieces[0].shape[0] // 2, pieces[0].shape[1]
    wide = 3 * PAIR
    height = PAIR // 2

    def kernel(places_ref, q_ref, k_ref, v_ref, mine_ref, over_ref, qkv_ref, far_ref):
        for i, ref in enumerate((q_ref, k_ref, v_ref)):
            qkv_ref[:features, i * PAIR : (i + 1) * PAIR] = ref[...]

        def write(x):
            for j, ref in enumerate((mine_ref, over_ref)):
                at = x ^ j
                qkv_ref[features + at * rows : features + (at + 1) * rows, :] = ref[:, :wide]
                for i in range(rows // height):
                    far_ref[at * height : (at + 1) * height, i * PAIR : (i + 1) * PAIR] = ref[
                        i * height : (i + 1) * height, wide:
                    ]

        for x in range(2):
            pl.when(places_ref[1] == x)(lambda x=x: write(x))

    column = pl.BlockSpec((features, PAIR), lambda i, p: (0, 2 * p[2] + p[0]))
    shapes = [(2 * features, wide), (PAIR, features)]
    return call(
        kernel,
        "join_heads",
        (1,),
        [column, column, column] + [pl.BlockSpec((rows, width), lambda i, p: (1, 0))] * 2,
        [whole(shape) for shape in shapes],
        [(shape, BF16) for shape in shapes],
        prefetch=1,
        after=after,
    )(places, w_query, w_key, w_value, *pieces)


def token_block(row_ref, count, step):
    return lax.rem(row_ref[0] + 2 * count - step, count)


def hidden_units(row, count, size, steps, blocks, w, b, earlier, after=()):
    features = blocks[0][0].shape[1]
    depth, width = w.shape
    number = 2 * len(steps)

    def kernel(row_ref, *refs):
        x_refs, refs = refs[: 2 * number], refs[2 * number :]
        w_ref, b_ref, (x_ref, hidden_ref, slope_ref) = refs[0], refs[1], refs[-3:]
        for i in range(number):

            @pl.when(pl.program_id(0) == i)
            def _(i=i):
                x_ref[:, :features] = x_refs[2 * i][...]
                x_ref[:, features:] = x_refs[2 * i + 1][...]

        u = mul(x_ref[...], w_ref[...], NN) + b_ref[...]
        scale = (2.0 / np.pi) ** 0.5
        square = u * u
        t = jnp.tanh(scale * u * (1.0 + 0.044715 * square))
        half = 0.5 * (1.0 + t)
        hidden_ref[...] = (u * half).astype(BF16)
        slope_ref[...] = half + 0.5 * u * (1.0 - t * t) * scale * (1.0 + 3 * 0.044715 * square)

    def at(i, row_ref):
        return (i % 2 * count + token_block(row_ref, count, steps[0] + i // 2), 0)

    rows = 2 * count * size
    shapes = [((rows, depth), BF16), ((rows, width), BF16), ((rows, width), F32)]
    return call(
        kernel,
        "hidden_units",
        (number,),
        [pl.BlockSpec((size, features), lambda i, r, n=n: (n, 0)) for _, n in blocks]
        + [whole((depth, width)), whole((1, width))]
        + [pl.BlockSpec(memory_space=pl.ANY)] * len(earlier),
        [pl.BlockSpec((size, shape[1]), at) for shape, _ in shapes],
        shapes,
        prefetch=1,
        after=after,
        aliases={3 + len(blocks) + i: i for i in range(len(earlier))},
    )(row, *(array for array, _ in blocks), w, b.reshape(1, -1), *earlier)


def take_half(both, after=()):
    size, width = both.shape[0] // 2, both.shape[1]

    def kernel(in_ref, out_ref):
        out_ref[...] = in_ref[...]

    return call(
        kernel,
        "take_half",
        (1,),
        [pl.BlockSpec((size, width), lambda i: (1, 0))],
        [whole((size, width))],
        [((size, width), BF16)],
        after=after,
    )(both)[0]


def outer(places, a, grads, after=()):
    rows, width = grads[0].shape
    units = a.shape[1]
    half = units // 2

    def kernel(places_ref, a0_ref, a1_ref, b0_ref, b1_ref, kept_ref, sent_ref):
        total = (mul(a0_ref[...], b0_ref[...], TN) + mul(a1_ref[...], b1_ref[...], TN)).astype(BF16)
        for x in range(2):

            @pl.when(places_ref[1] == x)
            def _(x=x):
                kept_ref[...] = total[x * half : (x + 1) * half]
                sent_ref[...] = total[(1 - x) * half : (2 - x) * half]

    return call(
        kernel,
        "outer",
        (1,),
        [pl.BlockSpec((rows, units), lambda i, p, s=s: (s, 0)) for s in range(2)]
        + [whole((rows, width))] * 2,
        [whole((half, width))] * 2,
        [((half, width), BF16)] * 2,
        prefetch=1,
        after=after,
    )(places, a, a, *grads)


def keep_tile(places_ref, i, total, near_ref, far_ref, sent_ref):
    total = total.astype(BF16)

    @pl.when(places_ref[1] == i % 2)
    def _():
        (near_ref, far_ref)[i // 2][...] = total

    @pl.when(places_ref[1] != i % 2)
    def _():
        sent_ref[i // 2] = total


def hidden_back(places, near, far, w_down, w_far, slope, x, after=()):
    rows, features = near[0].shape
    units = w_far.shape[0]
    size = rows // 2
    steps = 2 * rows // size
    tile = x.shape[1] // 4

    def kernel(places_ref, n0, n1, f0, f1, wn_ref, wf_ref, slope_ref, x_hbm, pre_ref, sum_ref, *refs):
        outs, (x_ref, sem) = refs[:-2], refs[-2:]
        i = pl.program_id(0)
        fetch = pltpu.make_async_copy(x_hbm, x_ref, sem)

        @pl.when(i == 0)
        def _():
            fetch.start()
            sum_ref[...] = jnp.zeros_like(sum_ref)

        def write(near_ref, far_ref):
            g = mul(near_ref[...], wn_ref[...], NT) + mul(far_ref[...], wf_ref[...], NT)
            g = (g * slope_ref[...]).astype(BF16)
            pre_ref[pl.ds(pl.multiple_of(i * size, size), size), :] = g
            sum_ref[...] += jnp.sum(g.astype(F32), axis=0, keepdims=True)

        pl.when(i < steps // 2)(lambda: write(n0, f0))
        pl.when(i >= steps // 2)(lambda: write(n1, f1))

        @pl.when(i == steps - 1)
        def _():
            fetch.wait()
            for j in range(4):
                keep_tile(places_ref, j, mul(x_ref[:, j * tile : (j + 1) * tile], pre_ref[...], TN), *outs)

    first = pl.BlockSpec((size, features), lambda i, p: (jnp.minimum(i, steps // 2 - 1), 0))
    second = pl.BlockSpec((size, features), lambda i, p: (jnp.maximum(i - steps // 2, 0), 0))
    shapes = [(tile, units), (tile, units), (2, tile, units)]
    return call(
        kernel,
        "hidden_back",
        (steps,),
        [first, second, first, second]
        + [pl.BlockSpec((units, features), lambda i, p: (2 * p[2] + p[0], 0)), whole(w_far.shape)]
        + [pl.BlockSpec((size, units), lambda i, p: (i, 0)), pl.BlockSpec(memory_space=pl.ANY)],
        [whole((2 * rows, units)), whole((1, units))] + [whole(shape) for shape in shapes],
        [((2 * rows, units), BF16), ((1, units), F32)] + [(shape, BF16) for shape in shapes],
        scratch=[pltpu.VMEM(x.shape, BF16), pltpu.SemaphoreType.DMA],
        prefetch=1,
        after=after,
    )(places, *near, *far, w_down, w_far, slope, x)


def ring_order(row_ref, count, target, sources):
    size = target.shape[0] // count
    for i in range(count):
        at = pl.ds(pl.multiple_of(token_block(row_ref, count, 1 + i) * size, size), size)
        left = 0
        for source in sources:
            width = source.shape[1]
            target[i * size : (i + 1) * size, left : left + width] = source[at, :]
            left += width


def back_to_tokens(row, count, side, pre, grads, up, qkv, after=()):
    rows = grads[0].shape[0]
    features = up.shape[0] // 2
    units, wide = pre.shape[1], grads[0].shape[1]
    depth = units + wide
    tile = 2 * TILE
    tiles = features // tile

    def kernel(row_ref, p0, p1, g0, g1, up_ref, qkv_ref, theirs_ref, own_ref, x_ref, w_ref):
        w_ref[:, :units] = up_ref[...]
        w_ref[:, units:] = qkv_ref[...]
        for s, (p, g, out_ref) in enumerate(((p1, g1, theirs_ref), (p0, g0, own_ref))):

            @pl.when(pl.program_id(0) == 0)
            def _(s=s, p=p, g=g):
                ring_order(row_ref, count, x_ref.at[s], (p, g))

            out_ref[...] = mul(x_ref[s], w_ref[...], NT).astype(BF16)

    return call(
        kernel,
        "back_to_tokens",
        (tiles,),
        [pl.BlockSpec((rows, units), lambda i, r, s=s: (s, 0)) for s in range(2)]
        + [whole(g.shape) for g in grads]
        + [pl.BlockSpec((tile, w.shape[1]), lambda i, r: (side * tiles + i, 0)) for w in (up, qkv)],
        [pl.BlockSpec((rows, tile), lambda i, r: (0, i))] * 2,
        [((rows, features), BF16)] * 2,
        scratch=[
            pltpu.VMEM((2, rows, depth), BF16),
            pltpu.VMEM((tile, depth), BF16),
        ],
        prefetch=1,
        after=after,
    )(row, pre, pre, *grads, up, qkv)


def mix(row, places, count, sequence, hidden, attended, w_down, down_far, w_out, out_far, after=()):
    units, features = down_far.shape
    rows = hidden.shape[0] // 2
    heads = out_far.shape[0]
    tile = 2 * TILE
    tiles = features // tile
    depth = units + heads

    def kernel(row_ref, p_ref, h_ref, a_ref, dn_ref, df_ref, on_ref, of_ref, out_ref, x_ref, w_ref):
        i = pl.program_id(0)

        @pl.when(i == 0)
        def _():
            ring_order(row_ref, count, x_ref, (h_ref, a_ref))

        @pl.when(i < tiles)
        def _():
            w_ref[:units] = dn_ref[...]
            w_ref[units:] = on_ref[...]

        @pl.when(i >= tiles)
        def _():
            w_ref[:units] = df_ref[...]
            w_ref[units:] = of_ref[...]

        out_ref[...] = mul(x_ref[...], w_ref[...], NN).astype(BF16)

    def near(height):
        return pl.BlockSpec((height, tile), lambda i, r, p: (2 * p[2] + p[0], jnp.minimum(i, tiles - 1)))

    def far(height):
        return pl.BlockSpec((height, tile), lambda i, r, p: (0, jnp.maximum(i - tiles, 0)))

    return call(
        kernel,
        "mix",
        (2 * tiles,),
        [pl.BlockSpec((rows, units), lambda i, r, p: (sequence, 0)), whole(attended.shape)]
        + [near(units), far(units), near(heads), far(heads)],
        [pl.BlockSpec((rows, tile), lambda i, r, p: (0, i))],
        [((rows, 2 * features), BF16)],
        scratch=[
            pltpu.VMEM((rows, depth), BF16),
            pltpu.VMEM((depth, tile), BF16),
        ],
        prefetch=2,
        after=after,
    )(row, places, hidden, attended, w_down, down_far, w_out, out_far)[0]


def add_blocks(kind, size, width, *terms, after=()):
    terms = [(*term, 0)[:3] for term in terms]

    def kernel(*refs):
        total = refs[0][...].astype(F32)
        for ref in refs[1:-1]:
            total = total + ref[...].astype(F32)
        refs[-1][...] = total.astype(kind)

    return call(
        kernel,
        "add_blocks",
        (1,),
        [pl.BlockSpec((size, width), lambda i, n=n, m=m: (n, m)) for _, n, m in terms],
        [whole((size, width))],
        [((size, width), kind)],
        after=after,
    )(*(array for array, _, _ in terms))[0]


def add_half(width, column, half, a, b, after=()):
    size = a.shape[0] // 4

    def kernel(a_ref, b_ref, out_ref):
        out_ref[...] = (a_ref[...].astype(F32) + b_ref[...].astype(F32)).astype(BF16)

    block = pl.BlockSpec((size, width), lambda i: (2 * half + i, column))
    return call(
        kernel,
        "add_half",
        (2,),
        [block, block],
        [pl.BlockSpec((size, width), lambda i: (i, 0))],
        [((2 * size, width), BF16)],
        after=after,
    )(a, b)[0]


def add_up(kind, *terms, after=()):
    def kernel(*refs):
        total = refs[0][...].astype(F32)
        for ref in refs[1:-1]:
            total = total + ref[...].astype(F32)
        refs[-1][...] = total.astype(kind)

    shape = terms[0].shape
    return call(
        kernel, "add_up", (1,), [whole(shape)] * len(terms), [whole(shape)], [(shape, kind)], after=after
    )(*terms)[0]


def add_pairs(kept, got, after=()):
    def kernel(near_ref, far_ref, got_ref, near_out, far_out):
        for i, (ref, out) in enumerate(((near_ref, near_out), (far_ref, far_out))):
            out[...] = (ref[...].astype(F32) + got_ref[i].astype(F32)).astype(BF16)

    shape = kept[0].shape
    return call(
        kernel,
        "add_pairs",
        (1,),
        [whole(shape), whole(shape), whole(got.shape)],
        [whole(shape)] * 2,
        [(shape, BF16)] * 2,
        after=after,
    )(*kept, got)


def rotary_rows(tokens):
    exponents = np.arange(0, ROT, 2).astype(np.float32) / np.float32(ROT)
    frequency = np.float32(10000.0) ** (-exponents)
    angles = (np.arange(tokens) % LEN).astype(np.float32)[:, None] * frequency[None, :]
    cosine, sine = np.cos(angles), np.sin(angles)
    none = np.zeros((tokens, ROT // 2), np.float32)
    rest = np.zeros((tokens, HEAD_DIM - ROT), np.float32)
    own = np.concatenate([cosine, cosine, rest + 1.0] * 2, axis=1)
    ahead = np.concatenate([-sine, none, rest] * 2, axis=1)
    behind = np.concatenate([none, sine, rest] * 2, axis=1)
    return tuple(table.astype(np.float32) for table in (own, ahead, behind))


def attention_kernel(
    sequence, places_ref, x_hbm, w_ref, bias_ref, near_hbm, far_hbm, on_ref, of_ref, own_ref, ahead_ref, behind_ref,
    *refs,
):
    *refs, x_ref, near_ref, far_ref, got_ref, sems, q_ref, k_ref, v_ref, d_ref, dq_ref, dk_ref, dv_ref = refs
    got_hbm = refs[0] if len(refs) == 7 else None
    out_ref, grad_ref, sum_ref, *weight_refs = refs if got_hbm is None else refs[1:]
    half = ROT // 2
    rows, features = near_hbm.shape
    own, ahead, behind = own_ref[...], ahead_ref[...], behind_ref[...]
    copies = [
        pltpu.make_async_copy(x_hbm.at[pl.ds(sequence * rows, rows)], x_ref, sems.at[0]),
        pltpu.make_async_copy(near_hbm, near_ref, sems.at[1]),
        pltpu.make_async_copy(far_hbm, far_ref, sems.at[2]),
    ]
    if got_hbm is not None:
        copies.append(pltpu.make_async_copy(got_hbm, got_ref, sems.at[3]))
    for copy in copies:
        copy.start()

    def turn(x):
        return x * own + pltpu.roll(x, PAIR - half, 1) * ahead + pltpu.roll(x, half, 1) * behind

    def turn_back(x):
        return x * own - pltpu.roll(x, PAIR - half, 1) * ahead - pltpu.roll(x, half, 1) * behind

    copies[0].wait()
    pre = mul(x_ref[...], w_ref[...], NN) + bias_ref[...]
    copies[1].wait()
    copies[2].wait()
    grad_out = mul(near_ref[...], on_ref[...], NT) + mul(far_ref[...], of_ref[...], NT)
    grad_out = grad_out.astype(BF16)
    biased = [pre[:, i * PAIR : (i + 1) * PAIR] for i in range(3)]
    query = turn(biased[0]).astype(BF16) * HEAD_DIM ** (-0.5)
    key = turn(biased[1]).astype(BF16)
    value = biased[2].astype(BF16)
    lane = lax.broadcasted_iota(jnp.int32, (rows, PAIR), 1)
    for head in range(2):
        mine = (lane >= head * HEAD_DIM) & (lane < (head + 1) * HEAD_DIM)
        for ref, array in ((q_ref, query), (k_ref, key), (v_ref, value), (d_ref, grad_out)):
            ref[head] = jnp.where(mine, array, jnp.zeros_like(array))

    tiles = rows // TILE
    for i in reversed(range(tiles)):
        at = pl.ds(i * TILE, TILE)
        span = (i + 1) * TILE
        attended = None
        grad_query = None
        for head in range(2):
            q, d = q_ref[head, at], d_ref[head, at]
            k, v = k_ref[head, :span], v_ref[head, :span]
            scores = mul(q, k, NT)
            row = lax.broadcasted_iota(jnp.int32, (TILE, span), 0) + i * TILE
            col = lax.broadcasted_iota(jnp.int32, (TILE, span), 1)
            scores = jnp.where(row >= col, scores, -1e30)
            e = jnp.exp(scores - jnp.max(scores, axis=1, keepdims=True))
            p = e * (1.0 / jnp.sum(e, axis=1, keepdims=True))
            w = p.astype(BF16)
            gw = mul(d, v, NT)
            gs = (p * (gw - jnp.sum(p * gw, axis=1, keepdims=True))).astype(BF16)
            o = mul(w, v, NN)
            gq = mul(gs, k, NN)
            attended = o if attended is None else attended + o
            grad_query = gq if grad_query is None else grad_query + gq
            gv = mul(w, d, TN)
            gk = mul(gs, q, TN)
            if i == tiles - 1 and head == 0:
                dv_ref[...] = gv
                dk_ref[...] = gk
            else:
                dv_ref[:span] += gv
                dk_ref[:span] += gk
        out_ref[at] = attended.astype(BF16)
        dq_ref[at] = grad_query
    gq = turn_back(dq_ref[...] * HEAD_DIM ** (-0.5)).astype(BF16)
    gk = turn_back(dk_ref[...]).astype(BF16)
    gv = dv_ref[...].astype(BF16)
    for i, g in enumerate((gq, gk, gv)):
        grad_ref[:, i * PAIR : (i + 1) * PAIR] = g
        sum_ref[:, i * PAIR : (i + 1) * PAIR] = jnp.sum(g.astype(F32), axis=0, keepdims=True)
    if got_hbm is not None:
        copies[3].wait()
    tile = 2 * features // 4
    for i in range(4):
        at = i * tile
        source = near_ref if at < features else far_ref
        block = jnp.concatenate(
            [
                mul(x_ref[:, at : at + tile], grad_ref[...], TN),
                mul(source[:, at % features : at % features + tile], out_ref[...], TN),
            ],
            axis=1,
        )
        if got_hbm is None:
            weight_refs[0][at : at + tile] = block.astype(BF16)
        else:
            keep_tile(places_ref, i, block + got_ref[at : at + tile].astype(F32), *weight_refs)


def attention(places, sequence, x, qkv, bias, near, far, w_out, out_far, earlier=None, after=()):
    rows, features = near.shape
    wide = 3 * PAIR
    tables = [jnp.asarray(table) for table in rotary_rows(rows)]
    tile = 2 * features // 4
    earlier = [] if earlier is None else [earlier]
    if earlier:
        shapes = [((tile, 4 * PAIR), BF16)] * 2 + [((2, tile, 4 * PAIR), BF16)]
    else:
        shapes = [((4 * tile, 4 * PAIR), BF16)]

    def kernel(*refs):
        attention_kernel(sequence, *refs)

    return call(
        kernel,
        "attention",
        (1,),
        [
            pl.BlockSpec(memory_space=pl.ANY),
            whole(qkv.shape),
            whole((1, wide)),
            pl.BlockSpec(memory_space=pl.ANY),
            pl.BlockSpec(memory_space=pl.ANY),
            pl.BlockSpec((PAIR, features), lambda i, p: (2 * p[2] + p[0], 0)),
            whole(out_far.shape),
        ]
        + [whole((rows, PAIR))] * 3
        + [pl.BlockSpec(memory_space=pl.ANY)] * len(earlier),
        [whole((rows, PAIR)), whole((rows, wide)), whole((1, wide))] + [whole(shape) for shape, _ in shapes],
        [((rows, PAIR), BF16), ((rows, wide), BF16), ((1, wide), F32)] + shapes,
        scratch=[pltpu.VMEM((rows, 2 * features), BF16)]
        + [pltpu.VMEM((rows, features), BF16)] * 2
        + [pltpu.VMEM((4 * tile, 4 * PAIR), BF16), pltpu.SemaphoreType.DMA((4,))]
        + [pltpu.VMEM((2, rows, PAIR), BF16)] * 4
        + [pltpu.VMEM((rows, PAIR), F32)] * 3,
        prefetch=1,
        after=after,
    )(places, x, qkv, bias.reshape(1, -1), near, far, w_out, out_far, *tables, *earlier)


def carry(array, after=()):
    def kernel(in_ref, out_ref):
        out_ref[...] = in_ref[...]

    half = pl.BlockSpec((array.shape[0] // 2, array.shape[1]), lambda i: (i, 0))
    return call(kernel, "carry", (2,), [half], [half], [(array.shape, array.dtype)], after=after)(array)[0]


def pair_up(first, second, after=()):
    shape = (2, *first.shape)

    def kernel(first_ref, second_ref, out_ref):
        for i, ref in enumerate((first_ref, second_ref)):

            @pl.when(pl.program_id(0) == i)
            def _(ref=ref):
                out_ref[0] = ref[...]

    return call(
        kernel,
        "pair_up",
        (2,),
        [whole(first.shape), whole(second.shape)],
        [pl.BlockSpec((1, *first.shape), lambda i: (i, 0, 0))],
        [(shape, first.dtype)],
        after=after,
    )(first, second)[0]


def place_kernel(places_ref, *refs):
    sources, targets = refs[:4], refs[4:]
    sibling, across, side = (pl.program_id(i) for i in range(3))
    for i in range(4):

        @pl.when((sibling == i // 2) & (across == i % 2))
        def _(source=sources[i]):
            block = source[side].astype(F32)
            if len(targets) == 1:
                targets[0][...] = block
            else:
                for t in range(3):
                    targets[t][...] = block[:, t * PAIR : (t + 1) * PAIR]
                targets[3][...] = block[:, 3 * PAIR :].T


def place(places, sources, blocks, shapes, maps, after=()):
    def spec(block, index):
        return pl.BlockSpec(block, lambda i, j, s, p: index(p[0] ^ i, p[1] ^ j, p[2] ^ s))

    return call(
        place_kernel,
        "place",
        (2, 2, 2),
        [whole(source.shape) for source in sources],
        [spec(*pair) for pair in zip(blocks, maps)],
        [(shape, F32) for shape in shapes],
        prefetch=1,
        after=after,
    )(places, *sources)


def swap(array, axis, bit=0, name="pieces"):
    size = lax.axis_size(axis)
    with jax.named_scope(name):
        return lax.ppermute(array, axis, [(i, i ^ (1 << bit)) for i in range(size)])


def step_up(array, name="row_ring"):
    size = lax.axis_size("row")
    with jax.named_scope(name):
        return lax.ppermute(array, "row", [(i, (i + 1) % size) for i in range(size)])


def part(array, index, parts, dim=0):
    size = array.shape[dim] // parts
    return lax.dynamic_slice_in_dim(array, index * size, size, dim)


def halves(array, dim):
    return jnp.split(array, 2, dim)


def pick(bit, first, second):
    return jnp.where(bit == 0, first, second)


def ordered(bit, mine, other, dim):
    return pick(bit, jnp.concatenate([mine, other], dim), jnp.concatenate([other, mine], dim))


def sync(*arrays):
    return lax.optimization_barrier(arrays)


def held(array, *others):
    return lax.optimization_barrier((array, *others))[0]


def add(a, b):
    return (a.astype(F32) + b.astype(F32)).astype(BF16)


def body(
    activations,
    ln_gain,
    ln_bias,
    w_query,
    w_key,
    w_value,
    b_query,
    b_key,
    b_value,
    w_out,
    w_up,
    b_up,
    w_down,
    out_bias,
    grad_out,
):
    dp, row, col = (lax.axis_index(axis) for axis in ("dp", "row", "col"))
    rows = lax.axis_size("row")
    bits = lax.axis_size("dp").bit_length() - 1
    places = [(dp >> bit) & 1 for bit in range(2)]
    where = jnp.stack([places[0], places[1], col]).astype(jnp.int32)
    here = row.reshape(1).astype(jnp.int32)
    own_rows, features = activations.shape
    feature_count = features * lax.axis_size("col")

    local = jnp.stack([jnp.sum(activations, axis=1), jnp.sum(activations * activations, axis=1)])
    early, third = cut_pieces(where, w_up, w_down, w_query, w_key, w_value, w_out)
    moments, early, third = sync(swap(local, "col"), early, third)
    moments = local + moments
    average = moments[0] / feature_count
    variance = moments[1] / feature_count - average * average
    inverse = lax.rsqrt(variance + 1e-05)[:, None]
    centered = (activations - average[:, None]) * inverse
    own = (centered * ln_gain + ln_bias).astype(BF16)

    def over_core(array, name="core"):
        return swap(array, "dp", 0, name)

    def over_x(array, name):
        return swap(array, "dp", 1, name)

    def over_col(array, name):
        return swap(array, "col", 0, name)

    biased = activations + out_bias

    near = [grad_out, over_core(grad_out, "grad_out")]
    own1 = step_up(own)
    other0 = over_col(own, "normed")
    early, other0 = sync(early, other0)
    early = over_col(early, "early")
    own2 = step_up(own1)
    front = jnp.concatenate([own, own1], 0)
    behind = jnp.concatenate([own2, other0], 0)
    ahead = step_up(behind)

    pieces = [early, over_x(early, "early")]
    up = join_up(where, w_up, pieces, after=near[1:])
    carried = carry(grad_out, after=[early])
    far = over_col(carried, "grad_out")
    other2 = step_up(take_half(ahead, after=[carried]))
    qkv, out_far = join_heads(where, w_query, w_key, w_value, pieces)
    third = over_col(third, "third")

    bias = [pick(places[0], *halves(b, 0)) for b in (b_query, b_key, b_value)]
    bias = jnp.concatenate(bias, 0)
    bias_up = pick(places[0], *halves(b_up, 0))

    front_sibling, behind_sibling, ahead_sibling = (
        over_core(a, "normed") for a in (front, behind, ahead)
    )
    blocks = [(front, 0), (behind, 1), (front_sibling, 0), (behind_sibling, 1)]
    blocks += [(front, 1), (ahead, 1), (front_sibling, 1), (ahead_sibling, 1)]
    normed, hidden, slope = hidden_units(
        here, rows, own_rows, range(2), blocks, up, bias_up, []
    )
    other2, hidden, qkv = sync(other2, hidden, qkv)
    other3 = step_up(other2)
    blocks = []
    for mine, late, sibling in ((behind, other2, behind_sibling), (ahead, other3, ahead_sibling)):
        blocks += [(mine, 0), (late, 0), (sibling, 0), (over_core(late, "normed"), 0)]
    normed, hidden, slope = hidden_units(
        here, rows, own_rows, range(2, rows), blocks, up, bias_up, [normed, hidden, slope]
    )

    def rest(total):
        for bit in range(2, bits):
            total = add(total, swap(total, "dp", bit))
        return total

    last = [hidden]

    def then(function, *arguments, pins=(), said=None):
        before = SAID[0]
        SAID[0] = before if said is None else said
        result = function(*arguments, after=[last[0], *pins])
        SAID[0] = before
        last[0] = jax.tree.leaves(result)[0]
        return result

    def plus(*terms, kind=BF16, pins=(), said=None):
        return then(
            lambda after: add_blocks(kind, own_rows, features, *terms, after=after), pins=pins, said=said
        )

    def plus_pairs(kept, got, pins=()):
        return [rest(total) for total in then(add_pairs, kept, got, pins=pins)]

    def attend(sequence, *arguments, pins=()):
        return then(
            lambda *a, after: attention(where, sequence, *a, after=after),
            normed, qkv, bias, near[sequence], far[sequence], w_out, out_far, *arguments, pins=pins,
        )

    def back(side, pins=()):
        return then(
            lambda *a, after: back_to_tokens(here, rows, side, *a, after=after),
            pre, qkv_grads, up, qkv, pins=pins,
        )

    def put(near, far, name, blocks, shapes, maps):
        pair = then(pair_up, near, far)
        across = over_x(pair, name)
        sources = [pair, across]

        def send():
            *sources[:], last[0] = sync(*sources, last[0])
            sources.extend(over_core(array, name) for array in sources[:])

        def write():
            return then(lambda *a, after: place(where, a, blocks, shapes, maps, after=after), *sources)

        return send, write, across

    def far_half(half, columns, own_terms, theirs, name):
        return over_col(
            then(lambda *a, after: add_half(features, columns, half, *a, after=after), own_terms, theirs), name
        )

    def outer_product(grads):
        return then(lambda *a, after: outer(where, *a, after=after), hidden, grads)

    far, last[0] = sync(far, last[0])
    far = [far, over_core(far, "grad_out")]
    attended0, grads0, sums0, weights = attend(0)
    third, last[0] = sync(third, last[0])
    third_across = over_x(third, "third")
    attended1, grads1, sums1, keep0, keep1, attn_send = attend(1, weights)
    attn_got = over_x(attn_send, "attn")
    qkv_grads = [grads0, grads1]

    down_far = then(lambda *a, after: join_down(where, *a, after=after), w_down, [third, third_across])

    def mixed_terms(sequence, attended):
        return then(
            lambda *a, after: mix(here, where, rows, sequence, *a, after=after),
            hidden, attended, w_down, down_far, w_out, out_far,
        )

    theirs = over_core(mixed_terms(1, attended1), "block_out")
    mixed = mixed_terms(0, attended0)
    out_first = far_half(0, 1, mixed, theirs, "block_out_col")

    pre, sum_up, up0, up1, up_send = then(
        lambda *a, after: hidden_back(where, *a, after=after), near, far, w_down, down_far, slope, normed
    )
    up_got = over_x(up_send, "up")
    attn_total = plus_pairs([keep0, keep1], attn_got)
    attn_mine = over_col(attn_total[1], "attn_far_col")

    near_terms, near_own = back(0)
    near_terms = over_core(near_terms, "grad_normed")
    far_terms, far_own = back(1)
    far_terms = over_core(far_terms, "grad_normed")
    mixed_next = step_up(
        plus((mixed, 0), (theirs, 0), (out_first, 0), pins=[attn_mine]), "block_out_ring"
    )
    SAID[0] = 1_300_000_000
    far_first = far_half(0, 0, far_own, far_terms, "grad_normed_col")

    near_keep, near_send = outer_product(near)
    near_got = over_x(near_send, "down_near")
    far_keep, far_send = outer_product(far)
    far_got = over_x(far_send, "down_far")

    up_total = plus_pairs([up0, up1], up_got, pins=[mixed_next])
    up_mine = over_col(up_total[1], "up_far_col")
    tall = attn_mine.shape[0]
    send_attn, put_attn, attn_across = put(
        attn_total[0], attn_mine,
        "attn_back",
        [(tall, PAIR)] * 3 + [(PAIR, tall)],
        [w_query.shape, w_key.shape, w_value.shape, w_out.shape],
        [lambda k, x, c: (x, c * 2 + k)] * 3 + [lambda k, x, c: (c * 2 + k, x)],
    )
    total = plus((near_own, 0), (near_terms, 0), (far_first, 0))
    total = step_up(total, "grad_normed_ring")
    far_second = far_half(1, 0, far_own, far_terms, "grad_normed_col")
    near_total = rest(plus((near_keep, 0), (near_got, 0)))
    far_total = rest(plus((far_keep, 0), (far_got, 0)))
    far_mine = over_col(far_total, "down_far_col")
    total = plus(
        (near_own, 1), (near_terms, 1), (far_first, 1), (total, 0), pins=[up_mine]
    )
    total = step_up(total, "grad_normed_ring")
    out_second = far_half(1, 1, mixed, theirs, "block_out_col")
    send_up, put_up, up_across = put(
        up_total[0], up_mine,
        "up_back",
        [up_mine.shape],
        [w_up.shape],
        [lambda k, x, c: (x, c * 2 + k)],
    )
    send_attn()
    total = plus((near_own, 2), (near_terms, 2), (far_second, 0), (total, 0), said=LARGE)
    total = step_up(total, "grad_normed_ring")
    mixed_next = step_up(plus((mixed, 1), (theirs, 1), (out_first, 1), (mixed_next, 0)), "block_out_ring")
    grad_w_query, grad_w_key, grad_w_value, grad_w_out = put_attn()
    send_down, put_down, down_across = put(
        near_total, far_mine,
        "down_back",
        [near_total.shape],
        [w_down.shape],
        [lambda k, x, c: (c * 4 + k * 2 + x, 0)],
    )
    send_up()
    grad_normed = plus(
        (near_own, 3), (near_terms, 3), (far_second, 1), (total, 0), kind=F32, said=LARGE
    )
    (grad_w_up,) = put_up()
    grad_normed, grad_w_up = sync(grad_normed, grad_w_up)
    mixed_next = step_up(
        plus((mixed, 2), (theirs, 2), (out_second, 0), (mixed_next, 0)), "block_out_ring"
    )
    send_down()
    (grad_w_down,) = put_down()
    block_out = plus(
        (mixed, 3), (theirs, 3), (out_second, 1), (mixed_next, 0), (biased, 0), kind=F32
    )
    SAID[0] = LARGE

    def over_all(array, axis, name):
        bits = lax.axis_size(axis).bit_length() - 1
        size = lax.axis_size(axis)
        for bit in range(0, bits, 2):
            masks = [1 << bit, 2 << bit, 3 << bit] if bit + 1 < bits else [1 << bit]
            with jax.named_scope(name):
                got = [lax.ppermute(array, axis, [(i, i ^ mask) for i in range(size)]) for mask in masks]
            array = array + got[0]
            if len(got) == 3:
                array = array + (got[1] + got[2])
        return array

    scaled = grad_normed * ln_gain
    local = jnp.stack([jnp.sum(scaled, axis=1), jnp.sum(scaled * centered, axis=1)])
    back_moments = (local + swap(local, "col", 0, "moments")) / feature_count
    own_grad = part(grad_out, row, rows).astype(F32)
    grad_activations = own_grad + inverse * (
        scaled - back_moments[0][:, None] - centered * back_moments[1][:, None]
    )
    grad_ln = jnp.stack([jnp.sum(grad_normed * centered, axis=0), jnp.sum(grad_normed, axis=0)])
    grad_ln = over_all(grad_ln, "row", "ln_row")

    sums = jnp.concatenate([sums0 + sums1, sum_up], 1)
    sums = ordered(places[0], sums, jnp.zeros_like(sums), 0)
    sizes = [grad_ln.size, sums.size]
    sums = jnp.concatenate([grad_ln.reshape(-1), sums.reshape(-1), jnp.sum(grad_out, axis=0, dtype=F32)])
    grad_ln, sums, grad_out_bias = jnp.split(over_all(sums, "dp", "sums"), [sizes[0], sum(sizes)])
    grad_ln, sums = grad_ln.reshape(2, -1), sums.reshape(2, -1)
    grad_bias = [sums[:, i * PAIR : (i + 1) * PAIR].reshape(-1) for i in range(3)]
    grad_b_up = sums[:, 3 * PAIR :].reshape(-1)


    return (
        block_out,
        grad_activations,
        grad_ln[0],
        grad_ln[1],
        grad_w_query,
        grad_w_key,
        grad_w_value,
        *grad_bias,
        grad_w_out,
        grad_w_up,
        grad_b_up,
        grad_w_down,
        grad_out_bias,
    )


def solution(mesh):
    placed = (
        P(("dp", "row"), "col"),
        P("col"),
        P("col"),
        P("col", "row"),
        P("col", "row"),
        P("col", "row"),
        P(("row", "col")),
        P(("row", "col")),
        P(("row", "col")),
        P("row", "col"),
        P("col", "row"),
        P(("row", "col")),
        P("row", "col"),
        P("col"),
        P("dp", "col"),
    )
    return jax.shard_map(
        body,
        mesh=mesh,
        in_specs=placed,
        out_specs=(
            P(("dp", "row"), "col"),
            P(("dp", "row"), "col"),
            P("col"),
            P("col"),
            P("col", "row"),
            P("col", "row"),
            P("col", "row"),
            P(("row", "col")),
            P(("row", "col")),
            P(("row", "col")),
            P("row", "col"),
            P("col", "row"),
            P(("row", "col")),
            P("row", "col"),
            P("col"),
        ),
        check_vma=False,
    )
```
